256 devices in a mesh: dom: 32 (over x, z), tp: 8 (over y, core).
Axes of the slice: x: 4, y: 4, z: 8, core: 2. Of those that a mesh axis runs over, the one named last changes fastest.
Arguments:
- queries: bfloat16 [512, 4, 8192], P('dom', None, 'tp'), may hold values from -100 to 100
- new_keys: bfloat16 [512, 4, 1024], P('dom', None, 'tp'), may hold values from -4 to 4
- new_values: bfloat16 [512, 4, 1024], P('dom', None, 'tp'), may hold values from -4 to 4
- prompt_keys: bfloat16 [2048, 1024], P(None, 'tp'), may hold values from -4 to 4
- prompt_values: bfloat16 [2048, 1024], P(None, 'tp'), may hold values from -4 to 4
- suffix_cache: bfloat16 [512, 2, 256, 1024], P('dom', None, None, 'tp'), may hold values from -4 to 4
- lengths: int32 [512], P('dom'), may hold values from 1 to 252
- ancestors: int32 [512], P('dom'), may hold values from 0 to 511, as said below
- out_weight: bfloat16 [8192, 4096], P('tp'), may hold values from -0.0625 to 0.0625
Outputs:
- mixed: bfloat16 [512, 4, 4096], P('dom', None, 'tp')
- new_cache: bfloat16 [512, 2, 256, 1024], P('dom', None, None, 'tp')
The draws below stay inside these ranges and needn't reach their ends.
Inputs may be any that keep to these rules, and one draw needn't show every extreme that they name: |ancestors[c] - c| <= 8 for every particle c.
All inputs are finite; a program needn't handle non-finite values.
Results may differ from the reference program's by a relative error of at most 0.019.
Values may be sent and summed in bfloat16 or wider, within the bound.
No kernel may reach another device: no remote copies, remote signals or barrier semaphores. Data moves between devices by JAX's collectives and lax.ppermute only.
A program may use at most 64 MiB of HBM per device.

```python
import math
import jax
import jax.numpy as jnp
from jax import lax

D = 4096
HQ = 64
KVH = 8
HD = 128
STEPS = 4
PROMPT = 2048
SUF = 256
P_DEV = 16
GROUP = 8
REACH = 8
PARTICLES = 512


def shared_keys(key):
    first, second = jax.random.split(key)
    prompt = jnp.clip(jax.random.normal(first, (PROMPT, KVH * HD), jnp.float32), -4.0, 4.0)
    fresh = jnp.clip(jax.random.normal(second, (PARTICLES, STEPS, KVH * HD), jnp.float32), -4.0, 4.0)
    return (prompt, fresh)


def draw_prompt_keys(key, part):
    prompt, fresh = shared_keys(key)
    return prompt.astype(jnp.bfloat16)


def draw_new_keys(key, part):
    prompt, fresh = shared_keys(key)
    return fresh.astype(jnp.bfloat16)


def draw_queries(key, part):
    prompt, fresh = shared_keys(key)
    key = jax.random.fold_in(key, 11)
    first = jax.random.fold_in(key, 0)
    noise = jnp.clip(jax.random.normal(first, (PARTICLES, STEPS, HQ * HD), jnp.float32), -4.0, 4.0)
    own = jnp.repeat(fresh.reshape(PARTICLES, STEPS, KVH, 1, HD), GROUP, axis=3)
    base = noise.reshape(PARTICLES, STEPS, HQ, HD) + 0.6 * own.reshape(PARTICLES, STEPS, HQ, HD)
    return base.reshape(PARTICLES, STEPS, HQ * HD).astype(jnp.bfloat16)


def draw_lengths(key, part):
    key = jax.random.fold_in(key, 5)
    first, second = jax.random.split(key)
    drawn = jax.random.randint(first, (PARTICLES,), 1, SUF - STEPS + 1)
    longest = jax.random.randint(second, (), 0, PARTICLES)
    return jnp.where(jnp.arange(PARTICLES) == longest, SUF - STEPS, drawn).astype(jnp.int32)


def draw_ancestors(key, part):
    key = jax.random.fold_in(key, 7)
    offsets = jax.random.randint(key, (PARTICLES,), -REACH, REACH + 1)
    index = jnp.arange(PARTICLES, dtype=jnp.int32)
    local = index % P_DEV
    device = index // P_DEV
    lower = jnp.logical_and(local == 0, device % 2 == 0)
    offsets = jnp.where(lower, -REACH, jnp.where(local == P_DEV - 1, REACH, offsets))
    return jnp.clip(index + offsets, 0, PARTICLES - 1).astype(jnp.int32)


def block_scale(stream_key, extent, shards, least, largest):
    def one(position, parts):
        draws = jax.random.uniform(jax.random.fold_in(jax.random.fold_in(stream_key, 6), position), (parts,), jnp.float32, least / len(shards), largest / len(shards))
        return jnp.repeat(jnp.exp(draws), extent[position] // parts).reshape((-1,) + (1,) * (len(extent) - position - 1))

    gain = one(*shards[0])
    for cut in shards[1:]:
        gain = gain * one(*cut)
    return gain


def scatter_about(own_key, extent, width, bound, cuts=(), kind=jnp.bfloat16):
    loudness = block_scale(own_key, extent, cuts, -0.22, 0.18) if cuts else 1.0
    values = jax.random.normal(own_key, extent, jnp.float32) * width * loudness
    return jnp.minimum(jnp.maximum(values, -bound), bound).astype(kind)


def setup_inputs(seed: int = 0) -> dict:
    key_list = jax.random.split(jax.random.key(seed), 10)
    return {
        "queries": draw_queries(jax.random.fold_in(key_list[9], 71), 0),
        "new_keys": draw_new_keys(jax.random.fold_in(key_list[9], 71), 0),
        "new_values": scatter_about(key_list[2], (PARTICLES, STEPS, KVH * HD), 1.0, 4.0, ((0, 32), (2, 8))),
        "prompt_keys": draw_prompt_keys(jax.random.fold_in(key_list[9], 71), 0),
        "prompt_values": scatter_about(key_list[4], (PROMPT, KVH * HD), 1.0, 4.0, ((1, 8),)),
        "suffix_cache": scatter_about(key_list[5], (PARTICLES, 2, SUF, KVH * HD), 1.0, 4.0, ((0, 32), (3, 8))),
        "lengths": draw_lengths(jax.random.fold_in(key_list[9], 71), 0),
        "ancestors": draw_ancestors(jax.random.fold_in(key_list[9], 71), 0),
        "out_weight": scatter_about(key_list[8], (HQ * HD, D), (HQ * HD) ** -0.5, 0.0625, ((0, 8),)),
    }


def attend_one(query, fresh_k, fresh_v, cache, length, prompt_keys, prompt_values):
    scale = 1.0 / math.sqrt(HD)
    query_heads = query.astype(jnp.float32).reshape(STEPS, KVH, GROUP, HD)
    prompt_k = prompt_keys.astype(jnp.float32).reshape(PROMPT, KVH, HD)
    cache_k = cache[0].astype(jnp.float32).reshape(SUF, KVH, HD)
    new_k = fresh_k.astype(jnp.float32).reshape(STEPS, KVH, HD)
    prompt_scores = jnp.einsum('sgqd,tgd->gqst', query_heads, prompt_k) * scale
    suffix_scores = jnp.einsum('sgqd,jgd->gqsj', query_heads, cache_k) * scale
    fresh_scores = jnp.einsum('sgqd,tgd->gqst', query_heads, new_k) * scale
    slots = jnp.arange(SUF, dtype=jnp.int32)
    suffix_scores = jnp.where(slots < length, suffix_scores, -jnp.inf)
    step_ids = jnp.arange(STEPS, dtype=jnp.int32)
    causal = step_ids[None, :] <= step_ids[:, None]
    fresh_scores = jnp.where(causal, fresh_scores, -jnp.inf)
    scores = jnp.concatenate([prompt_scores, suffix_scores, fresh_scores], axis=-1)
    top = lax.optimization_barrier(jnp.max(scores, axis=-1, keepdims=True))
    expo = jnp.exp(scores - top)
    weights = (expo / lax.optimization_barrier(jnp.sum(expo, axis=-1, keepdims=True))).astype(jnp.bfloat16)
    values = jnp.concatenate([prompt_values.reshape(PROMPT, KVH, HD), cache[1].reshape(SUF, KVH, HD), fresh_v.reshape(STEPS, KVH, HD)], axis=0).astype(jnp.float32)
    result = jnp.einsum('gqsc,cgd->sgqd', weights.astype(jnp.float32), values)
    return result.reshape(STEPS, HQ * HD).astype(jnp.bfloat16)

def reference(queries, new_keys, new_values, prompt_keys, prompt_values, suffix_cache, lengths, ancestors, out_weight):

    def per_particle(items):
        return attend_one(items[0], items[1], items[2], items[3], items[4], prompt_keys, prompt_values)
    attended = lax.map(per_particle, (queries, new_keys, new_values, suffix_cache, lengths))
    mixed = jnp.dot(attended.reshape(PARTICLES * STEPS, HQ * HD), out_weight, preferred_element_type=jnp.float32)
    mixed = mixed.astype(jnp.bfloat16).reshape(PARTICLES, STEPS, D)
    slots = jnp.arange(SUF, dtype=jnp.int32)
    fresh = jnp.stack((new_keys, new_values), axis=1)
    cache = suffix_cache
    for step in range(STEPS):
        chosen = slots[None, :] == lengths[:, None] + step
        cache = jnp.where(chosen[:, None, :, None], fresh[:, :, step][:, :, None, :], cache)
    live = slots[None, :] < lengths[:, None] + STEPS
    cache = jnp.where(live[:, None, :, None], cache, jnp.zeros((), jnp.bfloat16))
    new_cache = jnp.take(cache, ancestors.astype(jnp.int32), axis=0)
    return (mixed, new_cache)
```

```python
import functools
import math

import jax
import jax.numpy as jnp
from jax import lax
from jax.experimental import pallas as pl
from jax.experimental.pallas import tpu as pltpu
from jax.sharding import PartitionSpec as P

HD = 128
TILE = 16
F32 = jnp.float32
BF16 = jnp.bfloat16


def params(mib):
    return pltpu.CompilerParams(vmem_limit_bytes=mib * 1024 * 1024)


VMEM = pl.BlockSpec(memory_space=pltpu.VMEM)
SMEM = pl.BlockSpec(memory_space=pltpu.SMEM)
ANY = pl.BlockSpec(memory_space=pl.ANY)


def append_kernel(
    len_ref, anc_ref, cache_ref, nk_ref, nv_ref, app_ref, out_ref, in_sems, out_sems
):
    rows, _, slots, hd = app_ref.shape
    steps = nk_ref.shape[1]
    first = lax.axis_index("dom") * rows
    for p in range(rows):
        pltpu.make_async_copy(cache_ref.at[p], app_ref.at[p], in_sems.at[p]).start()
    span = 2 * TILE
    iota = lax.broadcasted_iota(jnp.int32, (span, hd), 0)
    for p in range(rows):
        pltpu.make_async_copy(cache_ref.at[p], app_ref.at[p], in_sems.at[p]).wait()
        length = len_ref[p]
        base = pl.multiple_of(jnp.minimum(length // TILE * TILE, slots - span), TILE)
        at = iota + (base - length)
        for kv, fresh_ref in ((0, nk_ref), (1, nv_ref)):
            fresh = fresh_ref[p].astype(F32)
            win = app_ref[p, kv, pl.ds(base, span), :].astype(F32)
            for t in range(steps):
                win = jnp.where(at == t, fresh[t : t + 1], win)
            win = jnp.where(at >= steps, 0.0, win)
            app_ref[p, kv, pl.ds(base, span), :] = win.astype(BF16)

        def clear(j, carry):
            row = pl.multiple_of(j * TILE, TILE)
            app_ref[p, :, pl.ds(row, TILE), :] = jnp.zeros((2, TILE, hd), BF16)
            return carry

        lax.fori_loop((base + span) // TILE, slots // TILE, clear, 0)
    for c in range(rows):
        local = anc_ref[c] - first

        @pl.when(jnp.logical_and(local >= 0, local < rows))
        def _():
            pltpu.make_async_copy(app_ref.at[local], out_ref.at[c], out_sems.at[c]).start()

    for c in range(rows):
        local = anc_ref[c] - first

        @pl.when(jnp.logical_and(local >= 0, local < rows))
        def _():
            pltpu.make_async_copy(app_ref.at[local], out_ref.at[c], out_sems.at[c]).wait()


def append(lengths, ancestors, cache, new_keys, new_values):
    rows = cache.shape[0]
    return pl.pallas_call(
        append_kernel,
        out_shape=(
            jax.ShapeDtypeStruct(cache.shape, BF16),
            jax.ShapeDtypeStruct(cache.shape, BF16),
        ),
        in_specs=[SMEM, SMEM, ANY, VMEM, VMEM],
        out_specs=(VMEM, ANY),
        scratch_shapes=[pltpu.SemaphoreType.DMA((rows,)), pltpu.SemaphoreType.DMA((rows,))],
        compiler_params=params(8),
        name="append",
    )(lengths, ancestors, cache, new_keys, new_values)


def attend_kernel(
    len_ref, q_ref, pk_ref, pv_ref, app_ref, w_ref, theirs_ref, ours_ref, qs, att, wbuf, sems
):
    rows, steps, _ = q_ref.shape
    heads = q_ref.shape[2] // HD
    slots = app_ref.shape[2]
    chips, tokens, width = theirs_ref.shape
    core = lax.rem(lax.axis_index("tp"), 2)

    def w_copy(k):
        who = 1 - core if k < chips else core
        block = 2 * (k % chips) + who
        cols = pl.ds(pl.multiple_of(block * width, width), width)
        return pltpu.make_async_copy(w_ref.at[:, cols], wbuf.at[k], sems.at[k])

    for k in range(2 * chips):
        w_copy(k).start()

    pair = 2 * steps
    groups = rows // 2
    block = heads * pair
    for g in range(groups):
        two = jnp.concatenate([q_ref[2 * g].astype(F32), q_ref[2 * g + 1].astype(F32)], 0)
        for h in range(heads):
            qs[pl.ds((g * heads + h) * pair, pair), :] = two[:, h * HD : (h + 1) * HD]

    factor = math.log2(math.e) / math.sqrt(HD)
    per = 2
    big = per * block
    prompt_k = pk_ref[...]
    prompt_v = pv_ref[...]
    r = lax.broadcasted_iota(jnp.int32, (pair, 2 * slots), 0)
    c = lax.broadcasted_iota(jnp.int32, (pair, 2 * slots), 1)
    same = (r // steps) == (c // slots)
    lead = lax.rem(c, slots) - lax.rem(r, steps)
    first = c < slots
    nt = (((1,), (1,)), ((), ()))
    for ch in range(groups // per):
        q = qs[pl.ds(ch * big, big), :].astype(BF16)
        s_prompt = lax.dot_general(q, prompt_k, nt, preferred_element_type=F32)
        s_own = []
        for i in range(per):
            g = ch * per + i
            keys = app_ref[2 * g : 2 * g + 2, 0].reshape(2 * slots, HD)
            s = lax.dot_general(
                q[i * block : (i + 1) * block], keys, nt, preferred_element_type=F32
            )
            limit = jnp.where(first, len_ref[2 * g], len_ref[2 * g + 1])
            seen = jnp.logical_and(same, lead <= limit)
            s = s.reshape(heads, pair, 2 * slots)
            s_own.append(jnp.where(seen[None], s, -1e30).reshape(block, 2 * slots))
        s_own = jnp.concatenate(s_own, 0)
        top = jnp.maximum(
            jnp.max(s_prompt, axis=1, keepdims=True), jnp.max(s_own, axis=1, keepdims=True)
        )
        e_prompt = jnp.exp2((s_prompt - top) * factor)
        e_own = jnp.exp2((s_own - top) * factor)
        total = jnp.sum(e_prompt, axis=1, keepdims=True) + jnp.sum(e_own, axis=1, keepdims=True)
        o = jnp.dot(e_prompt.astype(BF16), prompt_v, preferred_element_type=F32)
        e_own = e_own.astype(BF16)
        own = []
        for i in range(per):
            g = ch * per + i
            values = app_ref[2 * g : 2 * g + 2, 1].reshape(2 * slots, HD)
            own.append(
                jnp.dot(
                    e_own[i * block : (i + 1) * block], values, preferred_element_type=F32
                )
            )
        o = (o + jnp.concatenate(own, 0)) / total
        for i in range(per):
            g = ch * per + i
            for h in range(heads):
                at = i * block + h * pair
                att[pl.ds(g * pair, pair), h * HD : (h + 1) * HD] = o[at : at + pair]

    attended = att[...].astype(BF16)
    for k in range(2 * chips):
        w_copy(k).wait()
        part = jnp.dot(attended, wbuf[k], preferred_element_type=F32)
        if k < chips:
            theirs_ref[k] = part.astype(BF16)
        else:
            ours_ref[k - chips] = part


def attend(lengths, queries, prompt_keys, prompt_values, app, out_weight, chips, width):
    rows, steps, q_cols = queries.shape
    tokens = rows * steps
    flops = 2 * 2 * tokens * q_cols * prompt_keys.shape[0] + 2 * tokens * out_weight.size
    return pl.pallas_call(
        attend_kernel,
        out_shape=(
            jax.ShapeDtypeStruct((chips, tokens, width), BF16),
            jax.ShapeDtypeStruct((chips, tokens, width), F32),
        ),
        in_specs=[SMEM, VMEM, VMEM, VMEM, VMEM, ANY],
        out_specs=(VMEM, VMEM),
        scratch_shapes=[
            pltpu.VMEM((tokens * q_cols // HD, HD), F32),
            pltpu.VMEM((tokens, q_cols), F32),
            pltpu.VMEM((2 * chips, out_weight.shape[0], width), BF16),
            pltpu.SemaphoreType.DMA((2 * chips,)),
        ],
        compiler_params=params(28),
        cost_estimate=pl.CostEstimate(
            flops=flops, bytes_accessed=2 * out_weight.size, transcendentals=0
        ),
        name="attend",
    )(lengths, queries, prompt_keys, prompt_values, app, out_weight)


def pair_sum_kernel(ours_ref, got_ref, keep_ref, *send_refs):
    chips = ours_ref.shape[0]
    me = lax.axis_index("tp") // 2
    for k in range(chips):
        at = lax.rem(me + k, chips)
        both = ours_ref[at] + got_ref[at].astype(F32)
        if k == 0:
            keep_ref[...] = both
        else:
            send_refs[k - 1][...] = both.astype(BF16)


def pair_sum(ours, got):
    chips, tokens, width = ours.shape
    return pl.pallas_call(
        pair_sum_kernel,
        out_shape=(jax.ShapeDtypeStruct((tokens, width), F32),)
        + (jax.ShapeDtypeStruct((tokens, width), BF16),) * (chips - 1),
        in_specs=[VMEM, VMEM],
        out_specs=(VMEM,) * chips,
        compiler_params=params(4),
        name="pair_sum",
    )(ours, got)


def chip_sum_kernel(keep_ref, *refs):
    got_refs, out_ref = refs[:-1], refs[-1]
    rows, steps, _ = out_ref.shape
    total = keep_ref[...]
    for ref in got_refs:
        total = total + ref[...].astype(F32)
    total = total.astype(BF16)
    for p in range(rows):
        out_ref[p] = total[p * steps : (p + 1) * steps]


def chip_sum(keep, got, rows):
    tokens, width = keep.shape
    return pl.pallas_call(
        chip_sum_kernel,
        out_shape=jax.ShapeDtypeStruct((rows, tokens // rows, width), BF16),
        in_specs=[VMEM] * (1 + len(got)),
        out_specs=VMEM,
        compiler_params=params(2),
        name="chip_sum",
    )(keep, *got)


def place_kernel(anc_ref, a_ref, b_ref, held_ref, out_ref, sems):
    del held_ref
    rows = out_ref.shape[0]
    half = a_ref.shape[0]
    me = lax.axis_index("dom")
    even = lax.rem(me, 2) == 0

    def each(act):
        for c in range(rows):
            local = anc_ref[c] - me * rows
            above = local >= rows
            below = local < 0
            up = jnp.logical_and(above, even) | jnp.logical_and(below, jnp.logical_not(even))
            down = jnp.logical_and(below, even) | jnp.logical_and(above, jnp.logical_not(even))
            at = jnp.where(above, local - rows, local + half)
            at = jnp.clip(at, 0, half - 1)

            @pl.when(up)
            def _():
                act(pltpu.make_async_copy(a_ref.at[at], out_ref.at[c], sems.at[c]))

            @pl.when(down)
            def _():
                act(pltpu.make_async_copy(b_ref.at[at], out_ref.at[c], sems.at[c]))

    each(lambda copy: copy.start())
    each(lambda copy: copy.wait())


def place(ancestors, a, b, held):
    rows = held.shape[0]
    return pl.pallas_call(
        place_kernel,
        out_shape=jax.ShapeDtypeStruct(held.shape, BF16),
        in_specs=[SMEM, ANY, ANY, ANY],
        out_specs=ANY,
        scratch_shapes=[pltpu.SemaphoreType.DMA((rows,))],
        input_output_aliases={3: 0},
        compiler_params=params(1),
        name="place",
    )(ancestors, a, b, held)


def body(
    queries,
    new_keys,
    new_values,
    prompt_keys,
    prompt_values,
    suffix_cache,
    lengths,
    ancestors,
    out_weight,
):
    rows, steps, _ = queries.shape
    doms = lax.axis_size("dom")
    tps = lax.axis_size("tp")
    chips = tps // 2
    width = out_weight.shape[1] // tps
    half = rows // 2

    app, held = append(lengths, ancestors, suffix_cache, new_keys, new_values)
    even = lax.rem(lax.axis_index("dom"), 2) == 0
    low, high = app[:half], app[half:]
    pairs_a = [(i, i ^ 1) for i in range(doms)]
    pairs_b = [(i, i + 1) for i in range(1, doms - 1, 2)]
    pairs_b = pairs_b + [(j, i) for i, j in pairs_b]
    to_a = lax.dynamic_slice_in_dim(app, jnp.where(even, half, 0), half, 0)
    to_b = lax.dynamic_slice_in_dim(app, jnp.where(even, 0, half), half, 0)
    from_a = lax.ppermute(to_a, "dom", pairs_a)
    from_b = lax.ppermute(to_b, "dom", pairs_b)

    theirs, ours = attend(
        lengths, queries, prompt_keys, prompt_values, app, out_weight, chips, width
    )
    got = lax.ppermute(theirs, "tp", [(i, i ^ 1) for i in range(tps)])
    keep, *send = pair_sum(ours, got)
    arrived = [
        lax.ppermute(value, "tp", [(i, (i + 2 * k) % tps) for i in range(tps)])
        for k, value in enumerate(send, 1)
    ]
    mixed = chip_sum(keep, arrived, rows)
    new_cache = place(ancestors, from_a, from_b, held)
    return (mixed, new_cache)


def solution(mesh):
    in_specs = (
        P("dom", None, "tp"),
        P("dom", None, "tp"),
        P("dom", None, "tp"),
        P(None, "tp"),
        P(None, "tp"),
        P("dom", None, None, "tp"),
        P("dom"),
        P("dom"),
        P("tp", None),
    )
    out_specs = (P("dom", None, "tp"), P("dom", None, None, "tp"))
    return jax.shard_map(body, mesh=mesh, in_specs=in_specs, out_specs=out_specs, check_vma=False)
```

```python
import functools
import math

import jax
import jax.numpy as jnp
from jax import lax
from jax.experimental import pallas as pl
from jax.experimental.pallas import tpu as pltpu
from jax.sharding import PartitionSpec as P

HD = 128
TILE = 16
HEAD = 109
SLACK = HEAD - 15
F32 = jnp.float32
BF16 = jnp.bfloat16
VMEM = pl.BlockSpec(memory_space=pltpu.VMEM)
SMEM = pl.BlockSpec(memory_space=pltpu.SMEM)
HBM = pl.BlockSpec(memory_space=pltpu.HBM)
ANY = pl.BlockSpec(memory_space=pl.ANY)


def params(mib):
    return pltpu.CompilerParams(vmem_limit_bytes=mib * 1024 * 1024)


def in_hbm(value):
    return pltpu.with_memory_space_constraint(value, pltpu.HBM)


def like(value):
    return jax.ShapeDtypeStruct(value.shape, value.dtype)


def live_tiles(length, steps):
    return (length + steps + TILE - 1) // TILE


def tiles(first, count):
    return pl.ds(pl.multiple_of(first * TILE, TILE), pl.multiple_of(count * TILE, TILE))


def own_base(side, rows):
    even = lax.rem(lax.axis_index("dom"), 2) == 0
    return jnp.where(even, rows // 2 * (1 - side), rows // 2 * side)


def partner_of(side):
    me = lax.axis_index("dom")
    even = lax.rem(me, 2) == 0
    return jnp.where(even, me + 1 - 2 * side, me - 1 + 2 * side)


def assign(lens, base, places, steps):
    used = jnp.int32(1)
    for r in range(places.shape[0]):
        places[r] = used
        used = used + live_tiles(lens[base + r], steps)
    return used


def load_all(sources, targets, sems):
    copies = [
        pltpu.make_async_copy(a, b, sems.at[i]) for i, (a, b) in enumerate(zip(sources, targets))
    ]
    for copy in copies:
        copy.start()
    for copy in copies:
        copy.wait()


def tile_at(tile):
    return pl.ds(pl.multiple_of(tile * TILE, TILE), TILE)


def insert(target, at, tile, length, fresh, steps):
    line = lax.broadcasted_iota(jnp.int32, (TILE, HD), 0) + (tile * TILE - length)
    rows = target[at].astype(F32)
    for t in range(steps):
        rows = jnp.where(line == t, fresh[t : t + 1], rows)
    target[at] = jnp.where(line >= steps, 0.0, rows).astype(BF16)


def first_kernel(
    len_hbm, cache_ref, nk_hbm, nv_hbm, head_a, head_b, tail_a, tail_b,
    lens, nk, nv, place_a, place_b, spare, sems, head_sems, spare_sem,
):
    rows, kinds, slots, hd = cache_ref.shape
    half = rows // 2
    steps = nk.shape[1]
    copies = [
        pltpu.make_async_copy(a, b, sems.at[i])
        for i, (a, b) in enumerate(((len_hbm, lens), (nk_hbm, nk), (nv_hbm, nv)))
    ]
    for copy in copies:
        copy.start()
    copies[0].wait()
    sides = []
    for side, places, head, tail in ((0, place_a, head_a, tail_a), (1, place_b, head_b, tail_b)):
        base = own_base(side, rows)
        sides.append((side, base, assign(lens, base, places, steps), places, head, tail))

    def spots():
        for side, base, _, places, head, _ in sides:
            for r in range(half):
                count = live_tiles(lens[base + r], steps)
                copy = pltpu.make_async_copy(
                    cache_ref.at[base + r, :, tiles(0, count)],
                    head.at[:, tiles(places[r], count)],
                    head_sems.at[side, r],
                )
                yield places[r] + count <= HEAD, copy, base + r, count, places[r], head

    for fits, copy, *_ in spots():

        @pl.when(fits)
        def _():
            copy.start()

    for _, base, used, _, head, _ in sides:
        line = lax.broadcasted_iota(jnp.int32, (TILE, hd), 0)
        words = jnp.where(line == half, (used > HEAD).astype(jnp.int32), 0)
        for r in range(half):
            words = jnp.where(line == r, lens[base + r], words)
        head[0, :TILE, :] = words.astype(F32).astype(BF16)
    for copy in copies[1:]:
        copy.wait()

    def renew(target, place, p, count):
        for kv, fresh_ref in ((0, nk), (1, nv)):
            fresh = fresh_ref[p].astype(F32)
            for tile in (jnp.maximum(count - 2, 0), count - 1):
                insert(target, (kv, tile_at(place + tile)), tile, lens[p], fresh, steps)

    for fits, copy, p, count, place, head in spots():

        @pl.when(fits)
        def _():
            copy.wait()
            renew(head, place, p, count)

    for _, base, used, places, _, tail in sides:

        @pl.when(used > HEAD)
        def _():
            for r in range(half):
                count = live_tiles(lens[base + r], steps)
                place = places[r]

                @pl.when(place + count > HEAD)
                def _():
                    bring = pltpu.make_async_copy(cache_ref.at[base + r], spare, spare_sem.at[0])
                    bring.start()
                    bring.wait()
                    renew(spare, 0, base + r, count)
                    source = spare.at[:, tiles(0, count)]
                    target = tail.at[:, tiles(place - SLACK, count)]
                    leave = pltpu.make_async_copy(source, target, spare_sem.at[0])
                    leave.start()
                    leave.wait()


def first(lengths, cache, new_keys, new_values):
    rows, kinds, slots, hd = cache.shape
    half = rows // 2
    args = (lengths, cache, new_keys, new_values)
    head = jax.ShapeDtypeStruct((kinds, HEAD * TILE, hd), BF16)
    tail = jax.ShapeDtypeStruct((kinds, (half * slots // TILE + 1 - SLACK) * TILE, hd), BF16)
    return pl.pallas_call(
        first_kernel,
        out_shape=(
            head, head, tail, tail,
        ),
        in_specs=[HBM] * len(args),
        out_specs=(VMEM,) * 2 + (HBM,) * 2,
        scratch_shapes=[
            pltpu.SMEM((rows,), jnp.int32),
            pltpu.VMEM(new_keys.shape, BF16),
            pltpu.VMEM(new_values.shape, BF16),
            pltpu.SMEM((half,), jnp.int32),
            pltpu.SMEM((half,), jnp.int32),
            pltpu.VMEM(cache.shape[1:], BF16),
            pltpu.SemaphoreType.DMA((3,)),
            pltpu.SemaphoreType.DMA((2, half)),
            pltpu.SemaphoreType.DMA((1,)),
        ],
        compiler_params=params(4),
        name="first",
    )(*map(in_hbm, args))


def keep_kernel(steps, len_in, anc_in, app_ref, out_ref, lens, ancs, zero, live_sems, zero_sems, sems):
    rows, _, slots, _ = out_ref.shape
    first = lax.axis_index("dom") * rows
    zero[...] = jnp.zeros_like(zero)
    load_all((len_in, anc_in), (lens, ancs), sems)

    def each(act):
        @pl.loop(0, rows)
        def _(child):
            row = ancs[child] - first
            here = jnp.logical_and(row >= 0, row < rows)
            at = jnp.clip(row, 0, rows - 1)
            count = jnp.where(here, live_tiles(lens[at], steps), 0)
            rest = slots // TILE - count

            @pl.when(here)
            def _():
                part = tiles(0, count)
                source = app_ref.at[at, :, part]
                act(pltpu.make_async_copy(source, out_ref.at[child, :, part], live_sems.at[child]))

            @pl.when(rest > 0)
            def _():
                source = zero.at[:, tiles(0, rest)]
                target = out_ref.at[child, :, tiles(count, rest)]
                act(pltpu.make_async_copy(source, target, zero_sems.at[child]))

    each(lambda copy: copy.start())
    each(lambda copy: copy.wait())


def keep(steps, lengths, ancestors, app):
    rows = app.shape[0]
    return pl.pallas_call(
        functools.partial(keep_kernel, steps),
        out_shape=like(app),
        in_specs=[ANY, ANY, VMEM],
        out_specs=HBM,
        scratch_shapes=[
            pltpu.SMEM((rows,), jnp.int32),
            pltpu.SMEM((rows,), jnp.int32),
            pltpu.VMEM(app.shape[1:], BF16),
            pltpu.SemaphoreType.DMA((rows,)),
            pltpu.SemaphoreType.DMA((rows,)),
            pltpu.SemaphoreType.DMA((2,)),
        ],
        compiler_params=params(1),
        name="keep",
    )(lengths, ancestors, app)


def remote_rows(ancs, lens, places, rows, act):
    half = rows // 2
    me = lax.axis_index("dom")
    for side in range(2):
        partner = partner_of(side)
        children = jnp.where(partner > me, half, 0)
        for i in range(half):
            child = children + i
            row = ancs[child] - partner * rows - (half - children)

            @pl.when(jnp.logical_and(row >= 0, row < half))
            def _():
                act(child, side, lens[side, row], places[side, row])


def read_headers(header, lens, places, steps, most):
    half = lens.shape[1]
    for side in range(2):
        words = header[side].astype(F32)
        used = jnp.int32(1)
        for r in range(half):
            length = jnp.max(words[r : r + 1]).astype(jnp.int32)
            count = jnp.clip(live_tiles(length, steps), 1, most)
            lens[side, r] = count
            places[side, r] = used
            used = used + count


def place_kernel(
    steps, anc_in, sent_a, sent_b, head_a, head_b, held_ref, out_ref, any_ref, more_ref,
    ancs, lens, places, header, own, header_sems, live_sems,
):
    del held_ref
    rows, _, slots, _ = out_ref.shape
    top = pl.ds(0, TILE)
    load_all(
        (anc_in, head_a.at[0, top], head_b.at[0, top], sent_a.at[0, top], sent_b.at[0, top]),
        (ancs, header.at[0], header.at[1], own.at[0], own.at[1]),
        header_sems,
    )
    read_headers(header, lens, places, steps, slots // TILE)

    def each(act):
        def one(child, side, count, place):
            for which, head in enumerate((head_a, head_b)):

                if side != which:
                    continue

                @pl.when(place + count <= HEAD)
                def _():
                    source = head.at[:, tiles(place, count)]
                    target = out_ref.at[child, :, tiles(0, count)]
                    act(pltpu.make_async_copy(source, target, live_sems.at[child]))

        remote_rows(ancs, lens, places, rows, one)

    each(lambda copy: copy.start())
    flag = rows // 2
    both = jnp.maximum(header[...].astype(F32), own[...].astype(F32))
    for side in range(2):
        more_ref[side] = jnp.max(both[side, flag : flag + 1]).astype(jnp.int32)
    any_ref[0] = jnp.maximum(more_ref[0], more_ref[1])
    each(lambda copy: copy.wait())


def place(steps, ancestors, sent, heads, held):
    rows, _, _, hd = held.shape
    half = rows // 2
    return pl.pallas_call(
        functools.partial(place_kernel, steps),
        out_shape=(
            like(held),
            jax.ShapeDtypeStruct((1,), jnp.int32),
            jax.ShapeDtypeStruct((2,), jnp.int32),
        ),
        in_specs=[ANY] * 5 + [HBM],
        out_specs=(HBM, SMEM, SMEM),
        scratch_shapes=[
            pltpu.SMEM((rows,), jnp.int32),
            pltpu.SMEM((2, half), jnp.int32),
            pltpu.SMEM((2, half), jnp.int32),
            pltpu.VMEM((2, TILE, hd), BF16),
            pltpu.VMEM((2, TILE, hd), BF16),
            pltpu.SemaphoreType.DMA((5,)),
            pltpu.SemaphoreType.DMA((rows,)),
        ],
        input_output_aliases={5: 0},
        compiler_params=params(1),
        name="place",
    )(ancestors, *sent, *heads, in_hbm(held))


def place_tails_kernel(
    steps, anc_in, head_a, head_b, tail_a, tail_b, held_ref, out_ref,
    ancs, lens, places, header, header_sems, live_sems,
):
    del held_ref
    rows, _, slots, _ = out_ref.shape
    top = pl.ds(0, TILE)
    load_all(
        (anc_in, head_a.at[0, top], head_b.at[0, top]), (ancs, header.at[0], header.at[1]), header_sems
    )
    read_headers(header, lens, places, steps, slots // TILE)

    def each(act):
        def one(child, side, count, place):
            for which, tail in enumerate((tail_a, tail_b)):

                if side != which:
                    continue

                @pl.when(place + count > HEAD)
                def _():
                    source = tail.at[:, tiles(place - SLACK, count)]
                    target = out_ref.at[child, :, tiles(0, count)]
                    act(pltpu.make_async_copy(source, target, live_sems.at[child]))

        remote_rows(ancs, lens, places, rows, one)

    each(lambda copy: copy.start())
    each(lambda copy: copy.wait())


def place_tails(steps, ancestors, heads, tails, held):
    rows, _, _, hd = held.shape
    half = rows // 2
    return pl.pallas_call(
        functools.partial(place_tails_kernel, steps),
        out_shape=like(held),
        in_specs=[ANY] * 5 + [HBM],
        out_specs=HBM,
        scratch_shapes=[
            pltpu.SMEM((rows,), jnp.int32),
            pltpu.SMEM((2, half), jnp.int32),
            pltpu.SMEM((2, half), jnp.int32),
            pltpu.VMEM((2, TILE, hd), BF16),
            pltpu.SemaphoreType.DMA((3,)),
            pltpu.SemaphoreType.DMA((rows,)),
        ],
        input_output_aliases={5: 0},
        compiler_params=params(1),
        name="place_tails",
    )(ancestors, *heads, *tails, in_hbm(held))


def attend_kernel(
    len_in, cache_ref, nk_in, nv_in, q_ref, pk_ref, pv_ref, w_ref, theirs_ref, ours_ref, app_ref,
    len_ref, nk, nv, small_sems, in_sems, qs, att, wbuf, sems,
):
    rows, steps, _ = q_ref.shape
    heads = q_ref.shape[2] // HD
    slots = app_ref.shape[2]
    chips, tokens, width = theirs_ref.shape
    core = lax.rem(lax.axis_index("tp"), 2)

    def w_copy(k):
        who = jnp.where(k < chips, 1 - core, core)
        cols = pl.ds(pl.multiple_of((2 * lax.rem(k, chips) + who) * width, width), width)
        return pltpu.make_async_copy(w_ref.at[:, cols], wbuf.at[k], sems.at[k])

    @pl.loop(0, rows)
    def _(p):
        pltpu.make_async_copy(cache_ref.at[p], app_ref.at[p], in_sems.at[p]).start()

    @pl.loop(0, 2 * chips)
    def _(k):
        w_copy(k).start()

    load_all((len_in, nk_in, nv_in), (len_ref, nk, nv), small_sems)

    pair = 2 * steps
    groups = rows // 2
    block = heads * pair
    for g in range(groups):
        two = jnp.concatenate([q_ref[2 * g].astype(F32), q_ref[2 * g + 1].astype(F32)], 0)
        for h in range(heads):
            qs[pl.ds((g * heads + h) * pair, pair), :] = two[:, h * HD : (h + 1) * HD]

    for p in range(rows):
        pltpu.make_async_copy(cache_ref.at[p], app_ref.at[p], in_sems.at[p]).wait()
        count = live_tiles(len_ref[p], steps)
        for kv, fresh_ref in ((0, nk), (1, nv)):
            fresh = fresh_ref[p].astype(F32)
            for tile in (jnp.maximum(count - 2, 0), count - 1):
                insert(app_ref, (p, kv, tile_at(tile)), tile, len_ref[p], fresh, steps)

    factor = math.log2(math.e) / math.sqrt(HD)
    per = 4
    big = per * block
    prompt_k = pk_ref[...]
    prompt_v = pv_ref[...]
    r = lax.broadcasted_iota(jnp.int32, (pair, 2 * slots), 0)
    c = lax.broadcasted_iota(jnp.int32, (pair, 2 * slots), 1)
    same = (r // steps) == (c // slots)
    lead = jnp.where(same, lax.rem(c, slots) - lax.rem(r, steps), slots)
    left = c[:1] < slots
    nt = (((1,), (1,)), ((), ()))
    for ch in range(groups // per):
        q = qs[pl.ds(ch * big, big), :].astype(BF16)
        s_prompt = lax.dot_general(q, prompt_k, nt, preferred_element_type=F32)
        s_own = []
        for i in range(per):
            g = ch * per + i
            keys = app_ref[2 * g : 2 * g + 2, 0].reshape(2 * slots, HD)
            s = lax.dot_general(
                q[i * block : (i + 1) * block], keys, nt, preferred_element_type=F32
            )
            limit = jnp.where(left, len_ref[2 * g], len_ref[2 * g + 1])
            seen = lead <= limit
            s = s.reshape(heads, pair, 2 * slots)
            s_own.append(jnp.where(seen[None], s, -1e30).reshape(block, 2 * slots))
        s_own = jnp.concatenate(s_own, 0)
        top = jnp.maximum(
            jnp.max(s_prompt, axis=1, keepdims=True), jnp.max(s_own, axis=1, keepdims=True)
        )
        e_prompt = jnp.exp2((s_prompt - top) * factor)
        e_own = jnp.exp2((s_own - top) * factor)
        total = jnp.sum(e_prompt, axis=1, keepdims=True) + jnp.sum(e_own, axis=1, keepdims=True)
        o = jnp.dot(e_prompt.astype(BF16), prompt_v, preferred_element_type=F32)
        e_own = e_own.astype(BF16)
        own = []
        for i in range(per):
            g = ch * per + i
            values = app_ref[2 * g : 2 * g + 2, 1].reshape(2 * slots, HD)
            own.append(
                jnp.dot(
                    e_own[i * block : (i + 1) * block], values, preferred_element_type=F32
                )
            )
        o = (o + jnp.concatenate(own, 0)) / total
        for i in range(per):
            g = ch * per + i
            for h in range(heads):
                at = i * block + h * pair
                att[pl.ds(g * pair, pair), h * HD : (h + 1) * HD] = o[at : at + pair]

    attended = att[...].astype(BF16)
    for k in range(2 * chips):
        w_copy(jnp.int32(k)).wait()
        part = jnp.dot(attended, wbuf[k], preferred_element_type=F32)
        if k < chips:
            theirs_ref[k] = part.astype(BF16)
        else:
            ours_ref[k - chips] = part


def attend(
    lengths, cache, new_keys, new_values, queries, prompt_keys, prompt_values, out_weight, chips, width
):
    rows, steps, q_cols = queries.shape
    tokens = rows * steps
    flops = 2 * 2 * tokens * q_cols * prompt_keys.shape[0] + 2 * tokens * out_weight.size
    return pl.pallas_call(
        attend_kernel,
        out_shape=(
            jax.ShapeDtypeStruct((chips, tokens, width), BF16),
            jax.ShapeDtypeStruct((chips, tokens, width), F32),
            like(cache),
        ),
        in_specs=[ANY, HBM, ANY, ANY, VMEM, VMEM, VMEM, HBM],
        out_specs=(VMEM, VMEM, VMEM),
        scratch_shapes=[
            pltpu.SMEM((rows,), jnp.int32),
            pltpu.VMEM(new_keys.shape, BF16),
            pltpu.VMEM(new_values.shape, BF16),
            pltpu.SemaphoreType.DMA((3,)),
            pltpu.SemaphoreType.DMA((rows,)),
            pltpu.VMEM((tokens * q_cols // HD, HD), F32),
            pltpu.VMEM((tokens, q_cols), F32),
            pltpu.VMEM((2 * chips, out_weight.shape[0], width), BF16),
            pltpu.SemaphoreType.DMA((2 * chips,)),
        ],
        compiler_params=params(40),
        cost_estimate=pl.CostEstimate(
            flops=flops, bytes_accessed=2 * out_weight.size, transcendentals=0
        ),
        name="attend",
    )(
        lengths, in_hbm(cache), new_keys, new_values, queries, prompt_keys, prompt_values,
        in_hbm(out_weight),
    )


def pair_sum_kernel(ours_ref, got_ref, keep_ref, *send_refs):
    chips = ours_ref.shape[0]
    me = lax.axis_index("tp") // 2
    for k in range(chips):
        at = lax.rem(me + k, chips)
        both = ours_ref[at] + got_ref[at].astype(F32)
        if k == 0:
            keep_ref[...] = both
        else:
            send_refs[k - 1][...] = both.astype(BF16)


def pair_sum(ours, got):
    chips, tokens, width = ours.shape
    return pl.pallas_call(
        pair_sum_kernel,
        out_shape=(jax.ShapeDtypeStruct((tokens, width), F32),)
        + (jax.ShapeDtypeStruct((tokens, width), BF16),) * (chips - 1),
        in_specs=[VMEM, VMEM],
        out_specs=(VMEM,) * chips,
        compiler_params=params(2),
        name="pair_sum",
    )(ours, got)


def chip_sum_kernel(keep_ref, *refs):
    got_refs, out_ref = refs[:-1], refs[-1]
    rows, steps, _ = out_ref.shape
    total = keep_ref[...]
    for ref in got_refs:
        total = total + ref[...].astype(F32)
    total = total.astype(BF16)
    for p in range(rows):
        out_ref[p] = total[p * steps : (p + 1) * steps]


def chip_sum(keep, got, rows):
    tokens, width = keep.shape
    return pl.pallas_call(
        chip_sum_kernel,
        out_shape=jax.ShapeDtypeStruct((rows, tokens // rows, width), BF16),
        in_specs=[VMEM] * (1 + len(got)),
        out_specs=VMEM,
        compiler_params=params(2),
        name="chip_sum",
    )(keep, *got)


def body(
    queries,
    new_keys,
    new_values,
    prompt_keys,
    prompt_values,
    suffix_cache,
    lengths,
    ancestors,
    out_weight,
):
    rows, steps, _ = queries.shape
    doms = lax.axis_size("dom")
    tps = lax.axis_size("tp")
    chips = tps // 2
    width = out_weight.shape[1] // tps

    packed = first(lengths, suffix_cache, new_keys, new_values)
    even_pairs = [(i, i ^ 1) for i in range(doms)]
    odd_pairs = [(i, i + 1) for i in range(1, doms - 1, 2)]
    routes = (even_pairs, odd_pairs + [(j, i) for i, j in odd_pairs])
    heads = [lax.ppermute(head, "dom", route) for head, route in zip(packed[:2], routes)]

    theirs, ours, app = attend(
        lengths, suffix_cache, new_keys, new_values, queries, prompt_keys, prompt_values, out_weight,
        chips, width,
    )
    got = lax.ppermute(theirs, "tp", [(i, i ^ 1) for i in range(tps)])
    mine, *send = pair_sum(ours, got)
    arrived = [
        lax.ppermute(send[k - 1], "tp", [(i, (i + 2 * k) % tps) for i in range(tps)])
        for k in (2, 3, 1)
    ]
    mixed = chip_sum(mine, arrived, rows)
    held = keep(steps, lengths, ancestors, app)

    held, some, more = place(steps, ancestors, packed[:2], heads, held)

    def exchange(held, *tails):
        got = [
            lax.cond(
                flag > 0, lambda v, route=route: lax.ppermute(v, "dom", route), lambda v: v, tail
            )
            for flag, tail, route in zip((more[0], more[1]), tails, routes)
        ]
        return place_tails(steps, ancestors, heads, got, held)

    new_cache = lax.cond(some[0] > 0, exchange, lambda held, *tails: held, held, *packed[2:])
    return (mixed, new_cache)


def solution(mesh):
    in_specs = (
        P("dom", None, "tp"),
        P("dom", None, "tp"),
        P("dom", None, "tp"),
        P(None, "tp"),
        P(None, "tp"),
        P("dom", None, None, "tp"),
        P("dom"),
        P("dom"),
        P("tp", None),
    )
    out_specs = (P("dom", None, "tp"), P("dom", None, None, "tp"))
    return jax.shard_map(body, mesh=mesh, in_specs=in_specs, out_specs=out_specs, check_vma=False)
```

```python
import functools
import math

import jax
import jax.numpy as jnp
from jax import lax
from jax.experimental import pallas as pl
from jax.experimental.pallas import tpu as pltpu
from jax.sharding import PartitionSpec as P

HD = 128
TILE = 16
HEAD = 109
SLACK = HEAD - 15
F32 = jnp.float32
BF16 = jnp.bfloat16
VMEM = pl.BlockSpec(memory_space=pltpu.VMEM)
SMEM = pl.BlockSpec(memory_space=pltpu.SMEM)
HBM = pl.BlockSpec(memory_space=pltpu.HBM)
ANY = pl.BlockSpec(memory_space=pl.ANY)


def params(mib):
    return pltpu.CompilerParams(vmem_limit_bytes=mib * 1024 * 1024)


def in_hbm(value):
    return pltpu.with_memory_space_constraint(value, pltpu.HBM)


def like(value):
    return jax.ShapeDtypeStruct(value.shape, value.dtype)


def live_tiles(length, steps):
    return (length + steps + TILE - 1) // TILE


def tiles(first, count):
    return pl.ds(pl.multiple_of(first * TILE, TILE), pl.multiple_of(count * TILE, TILE))


def own_base(side, rows):
    even = lax.rem(lax.axis_index("dom"), 2) == 0
    return jnp.where(even, rows // 2 * (1 - side), rows // 2 * side)


def partner_of(side):
    me = lax.axis_index("dom")
    even = lax.rem(me, 2) == 0
    return jnp.where(even, me + 1 - 2 * side, me - 1 + 2 * side)


def assign(lens, base, places, steps):
    used = jnp.int32(1)
    for r in range(places.shape[0]):
        places[r] = used
        used = used + live_tiles(lens[base + r], steps)
    return used


def load_all(sources, targets, sems):
    copies = [
        pltpu.make_async_copy(a, b, sems.at[i]) for i, (a, b) in enumerate(zip(sources, targets))
    ]
    for copy in copies:
        copy.start()
    for copy in copies:
        copy.wait()


def tile_at(tile):
    return pl.ds(pl.multiple_of(tile * TILE, TILE), TILE)


def insert(target, at, tile, length, fresh, steps):
    line = lax.broadcasted_iota(jnp.int32, (TILE, HD), 0) + (tile * TILE - length)
    rows = target[at].astype(F32)
    for t in range(steps):
        rows = jnp.where(line == t, fresh[t : t + 1], rows)
    target[at] = jnp.where(line >= steps, 0.0, rows).astype(BF16)


def first_kernel(
    len_hbm, cache_ref, nk_hbm, nv_hbm, head_a, head_b, tail_a, tail_b,
    lens, nk, nv, place_a, place_b, spare, sems, head_sems, spare_sem,
):
    rows, kinds, slots, hd = cache_ref.shape
    half = rows // 2
    steps = nk.shape[1]
    copies = [
        pltpu.make_async_copy(a, b, sems.at[i])
        for i, (a, b) in enumerate(((len_hbm, lens), (nk_hbm, nk), (nv_hbm, nv)))
    ]
    for copy in copies:
        copy.start()
    copies[0].wait()
    sides = []
    for side, places, head, tail in ((0, place_a, head_a, tail_a), (1, place_b, head_b, tail_b)):
        base = own_base(side, rows)
        sides.append((side, base, assign(lens, base, places, steps), places, head, tail))

    def spots():
        for side, base, _, places, head, _ in sides:
            for r in range(half):
                count = live_tiles(lens[base + r], steps)
                copy = pltpu.make_async_copy(
                    cache_ref.at[base + r, :, tiles(0, count)],
                    head.at[:, tiles(places[r], count)],
                    head_sems.at[side, r],
                )
                yield places[r] + count <= HEAD, copy, base + r, count, places[r], head

    for fits, copy, *_ in spots():

        @pl.when(fits)
        def _():
            copy.start()

    for _, base, used, _, head, _ in sides:
        line = lax.broadcasted_iota(jnp.int32, (TILE, hd), 0)
        words = jnp.where(line == half, (used > HEAD).astype(jnp.int32), 0)
        for r in range(half):
            words = jnp.where(line == r, lens[base + r], words)
        head[0, :TILE, :] = words.astype(F32).astype(BF16)
    for copy in copies[1:]:
        copy.wait()

    def renew(target, place, p, count):
        for kv, fresh_ref in ((0, nk), (1, nv)):
            fresh = fresh_ref[p].astype(F32)
            for tile in (jnp.maximum(count - 2, 0), count - 1):
                insert(target, (kv, tile_at(place + tile)), tile, lens[p], fresh, steps)

    for fits, copy, p, count, place, head in spots():

        @pl.when(fits)
        def _():
            copy.wait()
            renew(head, place, p, count)

    for _, base, used, places, _, tail in sides:

        @pl.when(used > HEAD)
        def _():
            for r in range(half):
                count = live_tiles(lens[base + r], steps)
                place = places[r]

                @pl.when(place + count > HEAD)
                def _():
                    bring = pltpu.make_async_copy(cache_ref.at[base + r], spare, spare_sem.at[0])
                    bring.start()
                    bring.wait()
                    renew(spare, 0, base + r, count)
                    source = spare.at[:, tiles(0, count)]
                    target = tail.at[:, tiles(place - SLACK, count)]
                    leave = pltpu.make_async_copy(source, target, spare_sem.at[0])
                    leave.start()
                    leave.wait()


def first(lengths, cache, new_keys, new_values):
    rows, kinds, slots, hd = cache.shape
    half = rows // 2
    args = (lengths, cache, new_keys, new_values)
    head = jax.ShapeDtypeStruct((kinds, HEAD * TILE, hd), BF16)
    tail = jax.ShapeDtypeStruct((kinds, (half * slots // TILE + 1 - SLACK) * TILE, hd), BF16)
    return pl.pallas_call(
        first_kernel,
        out_shape=(
            head, head, tail, tail,
        ),
        in_specs=[HBM] * len(args),
        out_specs=(VMEM,) * 2 + (HBM,) * 2,
        scratch_shapes=[
            pltpu.SMEM((rows,), jnp.int32),
            pltpu.VMEM(new_keys.shape, BF16),
            pltpu.VMEM(new_values.shape, BF16),
            pltpu.SMEM((half,), jnp.int32),
            pltpu.SMEM((half,), jnp.int32),
            pltpu.VMEM(cache.shape[1:], BF16),
            pltpu.SemaphoreType.DMA((3,)),
            pltpu.SemaphoreType.DMA((2, half)),
            pltpu.SemaphoreType.DMA((1,)),
        ],
        compiler_params=params(4),
        name="first",
    )(*map(in_hbm, args))


def keep_kernel(steps, len_in, anc_in, app_ref, out_ref, lens, ancs, zero, live_sems, zero_sems, sems):
    rows, _, slots, _ = out_ref.shape
    first = lax.axis_index("dom") * rows
    zero[...] = jnp.zeros_like(zero)
    load_all((len_in, anc_in), (lens, ancs), sems)

    def each(act):
        @pl.loop(0, rows)
        def _(child):
            row = ancs[child] - first
            here = jnp.logical_and(row >= 0, row < rows)
            at = jnp.clip(row, 0, rows - 1)
            count = jnp.where(here, live_tiles(lens[at], steps), 0)
            rest = slots // TILE - count

            @pl.when(here)
            def _():
                part = tiles(0, count)
                source = app_ref.at[at, :, part]
                act(pltpu.make_async_copy(source, out_ref.at[child, :, part], live_sems.at[child]))

            @pl.when(rest > 0)
            def _():
                source = zero.at[:, tiles(0, rest)]
                target = out_ref.at[child, :, tiles(count, rest)]
                act(pltpu.make_async_copy(source, target, zero_sems.at[child]))

    each(lambda copy: copy.start())
    each(lambda copy: copy.wait())


def keep(steps, lengths, ancestors, app):
    rows = app.shape[0]
    return pl.pallas_call(
        functools.partial(keep_kernel, steps),
        out_shape=like(app),
        in_specs=[ANY, ANY, VMEM],
        out_specs=HBM,
        scratch_shapes=[
            pltpu.SMEM((rows,), jnp.int32),
            pltpu.SMEM((rows,), jnp.int32),
            pltpu.VMEM(app.shape[1:], BF16),
            pltpu.SemaphoreType.DMA((rows,)),
            pltpu.SemaphoreType.DMA((rows,)),
            pltpu.SemaphoreType.DMA((2,)),
        ],
        compiler_params=params(1),
        name="keep",
    )(lengths, ancestors, app)


def remote_rows(ancs, lens, places, rows, act):
    half = rows // 2
    me = lax.axis_index("dom")
    for side in range(2):
        partner = partner_of(side)
        children = jnp.where(partner > me, half, 0)
        for i in range(half):
            child = children + i
            row = ancs[child] - partner * rows - (half - children)

            @pl.when(jnp.logical_and(row >= 0, row < half))
            def _():
                act(child, side, lens[side, row], places[side, row])


def read_headers(header, lens, places, steps, most):
    half = lens.shape[1]
    for side in range(2):
        words = header[side].astype(F32)
        used = jnp.int32(1)
        for r in range(half):
            length = jnp.max(words[r : r + 1]).astype(jnp.int32)
            count = jnp.clip(live_tiles(length, steps), 1, most)
            lens[side, r] = count
            places[side, r] = used
            used = used + count


def place_kernel(
    steps, anc_in, sent_a, sent_b, head_a, head_b, held_ref, out_ref, any_ref, more_ref,
    ancs, lens, places, header, own, header_sems, live_sems,
):
    del held_ref
    rows, _, slots, _ = out_ref.shape
    top = pl.ds(0, TILE)
    load_all(
        (anc_in, head_a.at[0, top], head_b.at[0, top], sent_a.at[0, top], sent_b.at[0, top]),
        (ancs, header.at[0], header.at[1], own.at[0], own.at[1]),
        header_sems,
    )
    read_headers(header, lens, places, steps, slots // TILE)

    def each(act):
        def one(child, side, count, place):
            for which, head in enumerate((head_a, head_b)):

                if side != which:
                    continue

                @pl.when(place + count <= HEAD)
                def _():
                    source = head.at[:, tiles(place, count)]
                    target = out_ref.at[child, :, tiles(0, count)]
                    act(pltpu.make_async_copy(source, target, live_sems.at[child]))

        remote_rows(ancs, lens, places, rows, one)

    each(lambda copy: copy.start())
    flag = rows // 2
    both = jnp.maximum(header[...].astype(F32), own[...].astype(F32))
    for side in range(2):
        more_ref[side] = jnp.max(both[side, flag : flag + 1]).astype(jnp.int32)
    any_ref[0] = jnp.maximum(more_ref[0], more_ref[1])
    each(lambda copy: copy.wait())


def place(steps, ancestors, sent, heads, held):
    rows, _, _, hd = held.shape
    half = rows // 2
    return pl.pallas_call(
        functools.partial(place_kernel, steps),
        out_shape=(
            like(held),
            jax.ShapeDtypeStruct((1,), jnp.int32),
            jax.ShapeDtypeStruct((2,), jnp.int32),
        ),
        in_specs=[ANY] * 5 + [HBM],
        out_specs=(HBM, SMEM, SMEM),
        scratch_shapes=[
            pltpu.SMEM((rows,), jnp.int32),
            pltpu.SMEM((2, half), jnp.int32),
            pltpu.SMEM((2, half), jnp.int32),
            pltpu.VMEM((2, TILE, hd), BF16),
            pltpu.VMEM((2, TILE, hd), BF16),
            pltpu.SemaphoreType.DMA((5,)),
            pltpu.SemaphoreType.DMA((rows,)),
        ],
        input_output_aliases={5: 0},
        compiler_params=params(1),
        name="place",
    )(ancestors, *sent, *heads, in_hbm(held))


def place_tails_kernel(
    steps, anc_in, head_a, head_b, tail_a, tail_b, held_ref, out_ref,
    ancs, lens, places, header, header_sems, live_sems,
):
    del held_ref
    rows, _, slots, _ = out_ref.shape
    top = pl.ds(0, TILE)
    load_all(
        (anc_in, head_a.at[0, top], head_b.at[0, top]), (ancs, header.at[0], header.at[1]), header_sems
    )
    read_headers(header, lens, places, steps, slots // TILE)

    def each(act):
        def one(child, side, count, place):
            for which, tail in enumerate((tail_a, tail_b)):

                if side != which:
                    continue

                @pl.when(place + count > HEAD)
                def _():
                    source = tail.at[:, tiles(place - SLACK, count)]
                    target = out_ref.at[child, :, tiles(0, count)]
                    act(pltpu.make_async_copy(source, target, live_sems.at[child]))

        remote_rows(ancs, lens, places, rows, one)

    each(lambda copy: copy.start())
    each(lambda copy: copy.wait())


def place_tails(steps, ancestors, heads, tails, held):
    rows, _, _, hd = held.shape
    half = rows // 2
    return pl.pallas_call(
        functools.partial(place_tails_kernel, steps),
        out_shape=like(held),
        in_specs=[ANY] * 5 + [HBM],
        out_specs=HBM,
        scratch_shapes=[
            pltpu.SMEM((rows,), jnp.int32),
            pltpu.SMEM((2, half), jnp.int32),
            pltpu.SMEM((2, half), jnp.int32),
            pltpu.VMEM((2, TILE, hd), BF16),
            pltpu.SemaphoreType.DMA((3,)),
            pltpu.SemaphoreType.DMA((rows,)),
        ],
        input_output_aliases={5: 0},
        compiler_params=params(1),
        name="place_tails",
    )(ancestors, *heads, *tails, in_hbm(held))


def attend_kernel(
    len_in, cache_ref, nk_in, nv_in, q_ref, pk_ref, pv_ref, w_ref, theirs_ref, ours_ref, app_ref,
    len_ref, nk, nv, small_sems, in_sems, qs, att, wbuf, sems,
):
    rows, steps, _ = q_ref.shape
    heads = q_ref.shape[2] // HD
    slots = app_ref.shape[2]
    chips, tokens, width = theirs_ref.shape
    core = lax.rem(lax.axis_index("tp"), 2)

    def w_copy(k):
        who = jnp.where(k < chips, 1 - core, core)
        cols = pl.ds(pl.multiple_of((2 * lax.rem(k, chips) + who) * width, width), width)
        return pltpu.make_async_copy(w_ref.at[:, cols], wbuf.at[k], sems.at[k])

    @pl.loop(0, rows)
    def _(p):
        pltpu.make_async_copy(cache_ref.at[p], app_ref.at[p], in_sems.at[p]).start()

    @pl.loop(0, 2 * chips)
    def _(k):
        w_copy(k).start()

    load_all((len_in, nk_in, nv_in), (len_ref, nk, nv), small_sems)

    pair = 2 * steps
    groups = rows // 2
    block = heads * pair
    for g in range(groups):
        two = jnp.concatenate([q_ref[2 * g].astype(F32), q_ref[2 * g + 1].astype(F32)], 0)
        for h in range(heads):
            qs[pl.ds((g * heads + h) * pair, pair), :] = two[:, h * HD : (h + 1) * HD]

    for p in range(rows):
        pltpu.make_async_copy(cache_ref.at[p], app_ref.at[p], in_sems.at[p]).wait()
        count = live_tiles(len_ref[p], steps)
        for kv, fresh_ref in ((0, nk), (1, nv)):
            fresh = fresh_ref[p].astype(F32)
            for tile in (jnp.maximum(count - 2, 0), count - 1):
                insert(app_ref, (p, kv, tile_at(tile)), tile, len_ref[p], fresh, steps)

    factor = math.log2(math.e) / math.sqrt(HD)
    per = 4
    big = per * block
    prompt_k = pk_ref[...]
    prompt_v = pv_ref[...]
    r = lax.broadcasted_iota(jnp.int32, (pair, 2 * slots), 0)
    c = lax.broadcasted_iota(jnp.int32, (pair, 2 * slots), 1)
    same = (r // steps) == (c // slots)
    lead = jnp.where(same, lax.rem(c, slots) - lax.rem(r, steps), slots)
    left = c[:1] < slots
    nt = (((1,), (1,)), ((), ()))
    for ch in range(groups // per):
        q = qs[pl.ds(ch * big, big), :].astype(BF16)
        s_prompt = lax.dot_general(q, prompt_k, nt, preferred_element_type=F32)
        s_own = []
        for i in range(per):
            g = ch * per + i
            keys = app_ref[2 * g : 2 * g + 2, 0].reshape(2 * slots, HD)
            s = lax.dot_general(
                q[i * block : (i + 1) * block], keys, nt, preferred_element_type=F32
            )
            limit = jnp.where(left, len_ref[2 * g], len_ref[2 * g + 1])
            seen = lead <= limit
            s = s.reshape(heads, pair, 2 * slots)
            s_own.append(jnp.where(seen[None], s, -1e30).reshape(block, 2 * slots))
        s_own = jnp.concatenate(s_own, 0)
        top = jnp.maximum(
            jnp.max(s_prompt, axis=1, keepdims=True), jnp.max(s_own, axis=1, keepdims=True)
        )
        e_prompt = jnp.exp2((s_prompt - top) * factor)
        e_own = jnp.exp2((s_own - top) * factor)
        total = jnp.sum(e_prompt, axis=1, keepdims=True) + jnp.sum(e_own, axis=1, keepdims=True)
        o = jnp.dot(e_prompt.astype(BF16), prompt_v, preferred_element_type=F32)
        e_own = e_own.astype(BF16)
        own = []
        for i in range(per):
            g = ch * per + i
            values = app_ref[2 * g : 2 * g + 2, 1].reshape(2 * slots, HD)
            own.append(
                jnp.dot(
                    e_own[i * block : (i + 1) * block], values, preferred_element_type=F32
                )
            )
        o = (o + jnp.concatenate(own, 0)) / total
        for i in range(per):
            g = ch * per + i
            for h in range(heads):
                at = i * block + h * pair
                att[pl.ds(g * pair, pair), h * HD : (h + 1) * HD] = o[at : at + pair]

    attended = att[...].astype(BF16)
    for k in range(2 * chips):
        w_copy(jnp.int32(k)).wait()
        part = jnp.dot(attended, wbuf[k], preferred_element_type=F32)
        if k < chips:
            theirs_ref[k] = part.astype(BF16)
        else:
            ours_ref[k - chips] = part


def attend(
    lengths, cache, new_keys, new_values, queries, prompt_keys, prompt_values, out_weight, chips, width
):
    rows, steps, q_cols = queries.shape
    tokens = rows * steps
    flops = 2 * 2 * tokens * q_cols * prompt_keys.shape[0] + 2 * tokens * out_weight.size
    return pl.pallas_call(
        attend_kernel,
        out_shape=(
            jax.ShapeDtypeStruct((chips, tokens, width), BF16),
            jax.ShapeDtypeStruct((chips, tokens, width), F32),
            like(cache),
        ),
        in_specs=[ANY, HBM, ANY, ANY, VMEM, VMEM, VMEM, HBM],
        out_specs=(VMEM, VMEM, VMEM),
        scratch_shapes=[
            pltpu.SMEM((rows,), jnp.int32),
            pltpu.VMEM(new_keys.shape, BF16),
            pltpu.VMEM(new_values.shape, BF16),
            pltpu.SemaphoreType.DMA((3,)),
            pltpu.SemaphoreType.DMA((rows,)),
            pltpu.VMEM((tokens * q_cols // HD, HD), F32),
            pltpu.VMEM((tokens, q_cols), F32),
            pltpu.VMEM((2 * chips, out_weight.shape[0], width), BF16),
            pltpu.SemaphoreType.DMA((2 * chips,)),
        ],
        compiler_params=params(40),
        cost_estimate=pl.CostEstimate(
            flops=flops, bytes_accessed=2 * out_weight.size, transcendentals=0
        ),
        name="attend",
    )(
        lengths, in_hbm(cache), new_keys, new_values, queries, prompt_keys, prompt_values,
        in_hbm(out_weight),
    )


def pair_sum_kernel(ours_ref, got_ref, keep_ref, *send_refs):
    chips = ours_ref.shape[0]
    me = lax.axis_index("tp") // 2
    for k in range(chips):
        at = lax.rem(me + k, chips)
        both = ours_ref[at] + got_ref[at].astype(F32)
        if k == 0:
            keep_ref[...] = both
        else:
            send_refs[k - 1][...] = both.astype(BF16)


def pair_sum(ours, got):
    chips, tokens, width = ours.shape
    return pl.pallas_call(
        pair_sum_kernel,
        out_shape=(jax.ShapeDtypeStruct((tokens, width), F32),)
        + (jax.ShapeDtypeStruct((tokens, width), BF16),) * (chips - 1),
        in_specs=[VMEM, VMEM],
        out_specs=(VMEM,) * chips,
        compiler_params=params(2),
        name="pair_sum",
    )(ours, got)


def chip_sum_kernel(keep_ref, *refs):
    got_refs, out_ref = refs[:-1], refs[-1]
    rows, steps, _ = out_ref.shape
    total = keep_ref[...]
    for ref in got_refs:
        total = total + ref[...].astype(F32)
    total = total.astype(BF16)
    for p in range(rows):
        out_ref[p] = total[p * steps : (p + 1) * steps]


def chip_sum(keep, got, rows):
    tokens, width = keep.shape
    return pl.pallas_call(
        chip_sum_kernel,
        out_shape=jax.ShapeDtypeStruct((rows, tokens // rows, width), BF16),
        in_specs=[VMEM] * (1 + len(got)),
        out_specs=VMEM,
        compiler_params=params(2),
        name="chip_sum",
    )(keep, *got)


def body(
    queries,
    new_keys,
    new_values,
    prompt_keys,
    prompt_values,
    suffix_cache,
    lengths,
    ancestors,
    out_weight,
):
    rows, steps, _ = queries.shape
    doms = lax.axis_size("dom")
    tps = lax.axis_size("tp")
    chips = tps // 2
    width = out_weight.shape[1] // tps

    packed = first(lengths, suffix_cache, new_keys, new_values)
    def partner(i, side):
        dom, tp = divmod(i, tps)
        other = dom ^ 1 if side == 0 else (dom + 1) // 2 * 4 - 1 - dom
        return other * tps + tp if 0 <= other < doms else i ^ 1

    routes = [[(i, partner(i, side)) for i in range(doms * tps)] for side in range(2)]
    heads = [lax.ppermute(head, ("dom", "tp"), route) for head, route in zip(packed[:2], routes)]

    theirs, ours, app = attend(
        lengths, suffix_cache, new_keys, new_values, queries, prompt_keys, prompt_values, out_weight,
        chips, width,
    )
    got = lax.ppermute(theirs, "tp", [(i, i ^ 1) for i in range(tps)])
    mine, *send = pair_sum(ours, got)
    arrived = [
        lax.ppermute(send[k - 1], "tp", [(i, (i + 2 * k) % tps) for i in range(tps)])
        for k in (2, 3, 1)
    ]
    mixed = chip_sum(mine, arrived, rows)
    held = keep(steps, lengths, ancestors, app)

    held, some, more = place(steps, ancestors, packed[:2], heads, held)

    def exchange(held, *tails):
        got = [
            lax.cond(
                flag > 0, lambda v, route=route: lax.ppermute(v, ("dom", "tp"), route), lambda v: v, tail
            )
            for flag, tail, route in zip((more[0], more[1]), tails, routes)
        ]
        return place_tails(steps, ancestors, heads, got, held)

    new_cache = lax.cond(some[0] > 0, exchange, lambda held, *tails: held, held, *packed[2:])
    return (mixed, new_cache)


def solution(mesh):
    in_specs = (
        P("dom", None, "tp"),
        P("dom", None, "tp"),
        P("dom", None, "tp"),
        P(None, "tp"),
        P(None, "tp"),
        P("dom", None, None, "tp"),
        P("dom"),
        P("dom"),
        P("tp", None),
    )
    out_specs = (P("dom", None, "tp"), P("dom", None, None, "tp"))
    return jax.shard_map(body, mesh=mesh, in_specs=in_specs, out_specs=out_specs, check_vma=False)
```

```python
import functools
import math

import jax
import jax.numpy as jnp
from jax import lax
from jax.experimental import pallas as pl
from jax.experimental.pallas import tpu as pltpu
from jax.sharding import PartitionSpec as P

HD = 128
TILE = 16
HEAD = 109
SLACK = HEAD - 15
F32 = jnp.float32
BF16 = jnp.bfloat16
VMEM = pl.BlockSpec(memory_space=pltpu.VMEM)
SMEM = pl.BlockSpec(memory_space=pltpu.SMEM)
HBM = pl.BlockSpec(memory_space=pltpu.HBM)
ANY = pl.BlockSpec(memory_space=pl.ANY)


def params(mib):
    return pltpu.CompilerParams(vmem_limit_bytes=mib * 1024 * 1024)


def in_hbm(value):
    return pltpu.with_memory_space_constraint(value, pltpu.HBM)


def like(value):
    return jax.ShapeDtypeStruct(value.shape, value.dtype)


def live_tiles(length, steps):
    return (length + steps + TILE - 1) // TILE


def tiles(first, count):
    return pl.ds(pl.multiple_of(first * TILE, TILE), pl.multiple_of(count * TILE, TILE))


def own_base(side, rows):
    even = lax.rem(lax.axis_index("dom"), 2) == 0
    return jnp.where(even, rows // 2 * (1 - side), rows // 2 * side)


def partner_of(side):
    me = lax.axis_index("dom")
    even = lax.rem(me, 2) == 0
    return jnp.where(even, me + 1 - 2 * side, me - 1 + 2 * side)


def assign(lens, base, places, steps):
    used = jnp.int32(1)
    for r in range(places.shape[0]):
        places[r] = used
        used = used + live_tiles(lens[base + r], steps)
    return used


def load_all(sources, targets, sems):
    copies = [
        pltpu.make_async_copy(a, b, sems.at[i]) for i, (a, b) in enumerate(zip(sources, targets))
    ]
    for copy in copies:
        copy.start()
    for copy in copies:
        copy.wait()


def tile_at(tile):
    return pl.ds(pl.multiple_of(tile * TILE, TILE), TILE)


def insert(target, at, tile, length, fresh, steps):
    line = lax.broadcasted_iota(jnp.int32, (TILE, HD), 0) + (tile * TILE - length)
    rows = target[at].astype(F32)
    for t in range(steps):
        rows = jnp.where(line == t, fresh[t : t + 1], rows)
    target[at] = jnp.where(line >= steps, 0.0, rows).astype(BF16)


def first_kernel(
    len_hbm, cache_ref, nk_hbm, nv_hbm, head_a, head_b, tail_a, tail_b,
    lens, nk, nv, place_a, place_b, spare, sems, head_sems, spare_sem,
):
    rows, kinds, slots, hd = cache_ref.shape
    half = rows // 2
    steps = nk.shape[1]
    copies = [
        pltpu.make_async_copy(a, b, sems.at[i])
        for i, (a, b) in enumerate(((len_hbm, lens), (nk_hbm, nk), (nv_hbm, nv)))
    ]
    for copy in copies:
        copy.start()
    copies[0].wait()
    sides = []
    for side, places, head, tail in ((0, place_a, head_a, tail_a), (1, place_b, head_b, tail_b)):
        base = own_base(side, rows)
        sides.append((side, base, assign(lens, base, places, steps), places, head, tail))

    def spots():
        for side, base, _, places, head, _ in sides:
            for r in range(half):
                count = live_tiles(lens[base + r], steps)
                copy = pltpu.make_async_copy(
                    cache_ref.at[base + r, :, tiles(0, count)],
                    head.at[:, tiles(places[r], count)],
                    head_sems.at[side, r],
                )
                yield places[r] + count <= HEAD, copy, base + r, count, places[r], head

    for fits, copy, *_ in spots():

        @pl.when(fits)
        def _():
            copy.start()

    for _, base, used, _, head, _ in sides:
        line = lax.broadcasted_iota(jnp.int32, (TILE, hd), 0)
        words = jnp.where(line == half, (used > HEAD).astype(jnp.int32), 0)
        for r in range(half):
            words = jnp.where(line == r, lens[base + r], words)
        head[0, :TILE, :] = words.astype(F32).astype(BF16)
    for copy in copies[1:]:
        copy.wait()

    def renew(target, place, p, count):
        def one(tile):
            for kv, fresh_ref in ((0, nk), (1, nv)):
                fresh = fresh_ref[p].astype(F32)
                insert(target, (kv, tile_at(place + tile)), tile, lens[p], fresh, steps)

        one(count - 1)

        @pl.when(lens[p] < (count - 1) * TILE)
        def _():
            one(count - 2)

    for fits, copy, p, count, place, head in spots():

        @pl.when(fits)
        def _():
            copy.wait()
            renew(head, place, p, count)

    for _, base, used, places, _, tail in sides:

        @pl.when(used > HEAD)
        def _():
            for r in range(half):
                count = live_tiles(lens[base + r], steps)
                place = places[r]

                @pl.when(place + count > HEAD)
                def _():
                    bring = pltpu.make_async_copy(cache_ref.at[base + r], spare, spare_sem.at[0])
                    bring.start()
                    bring.wait()
                    renew(spare, 0, base + r, count)
                    source = spare.at[:, tiles(0, count)]
                    target = tail.at[:, tiles(place - SLACK, count)]
                    leave = pltpu.make_async_copy(source, target, spare_sem.at[0])
                    leave.start()
                    leave.wait()


def first(lengths, cache, new_keys, new_values):
    rows, kinds, slots, hd = cache.shape
    half = rows // 2
    args = (lengths, cache, new_keys, new_values)
    head = jax.ShapeDtypeStruct((kinds, HEAD * TILE, hd), BF16)
    tail = jax.ShapeDtypeStruct((kinds, (half * slots // TILE + 1 - SLACK) * TILE, hd), BF16)
    return pl.pallas_call(
        first_kernel,
        out_shape=(
            head, head, tail, tail,
        ),
        in_specs=[HBM] * len(args),
        out_specs=(VMEM,) * 2 + (HBM,) * 2,
        scratch_shapes=[
            pltpu.SMEM((rows,), jnp.int32),
            pltpu.VMEM(new_keys.shape, BF16),
            pltpu.VMEM(new_values.shape, BF16),
            pltpu.SMEM((half,), jnp.int32),
            pltpu.SMEM((half,), jnp.int32),
            pltpu.VMEM(cache.shape[1:], BF16),
            pltpu.SemaphoreType.DMA((3,)),
            pltpu.SemaphoreType.DMA((2, half)),
            pltpu.SemaphoreType.DMA((1,)),
        ],
        compiler_params=params(4),
        name="first",
    )(*map(in_hbm, args))


def keep_kernel(steps, len_in, anc_in, app_ref, out_ref, lens, ancs, zero, live_sems, zero_sems, sems):
    rows, _, slots, _ = out_ref.shape
    first = lax.axis_index("dom") * rows
    zero[...] = jnp.zeros_like(zero)
    load_all((len_in, anc_in), (lens, ancs), sems)

    def each(act):
        @pl.loop(0, rows)
        def _(child):
            row = ancs[child] - first
            here = jnp.logical_and(row >= 0, row < rows)
            at = jnp.clip(row, 0, rows - 1)
            count = jnp.where(here, live_tiles(lens[at], steps), 0)
            rest = slots // TILE - count

            @pl.when(here)
            def _():
                part = tiles(0, count)
                source = app_ref.at[at, :, part]
                act(pltpu.make_async_copy(source, out_ref.at[child, :, part], live_sems.at[child]))

            @pl.when(rest > 0)
            def _():
                source = zero.at[:, tiles(0, rest)]
                target = out_ref.at[child, :, tiles(count, rest)]
                act(pltpu.make_async_copy(source, target, zero_sems.at[child]))

    each(lambda copy: copy.start())
    each(lambda copy: copy.wait())


def keep(steps, lengths, ancestors, app):
    rows = app.shape[0]
    return pl.pallas_call(
        functools.partial(keep_kernel, steps),
        out_shape=like(app),
        in_specs=[ANY, ANY, VMEM],
        out_specs=HBM,
        scratch_shapes=[
            pltpu.SMEM((rows,), jnp.int32),
            pltpu.SMEM((rows,), jnp.int32),
            pltpu.VMEM(app.shape[1:], BF16),
            pltpu.SemaphoreType.DMA((rows,)),
            pltpu.SemaphoreType.DMA((rows,)),
            pltpu.SemaphoreType.DMA((2,)),
        ],
        compiler_params=params(1),
        name="keep",
    )(lengths, ancestors, app)


def remote_rows(ancs, lens, places, rows, act):
    half = rows // 2
    me = lax.axis_index("dom")
    for side in range(2):
        partner = partner_of(side)
        children = jnp.where(partner > me, half, 0)
        for i in range(half):
            child = children + i
            row = ancs[child] - partner * rows - (half - children)

            @pl.when(jnp.logical_and(row >= 0, row < half))
            def _():
                act(child, side, lens[side, row], places[side, row])


def read_headers(header, lens, places, steps, most):
    half = lens.shape[1]
    for side in range(2):
        words = header[side].astype(F32)
        used = jnp.int32(1)
        for r in range(half):
            length = jnp.max(words[r : r + 1]).astype(jnp.int32)
            count = jnp.clip(live_tiles(length, steps), 1, most)
            lens[side, r] = count
            places[side, r] = used
            used = used + count


def place_kernel(
    steps, anc_in, sent_a, sent_b, head_a, head_b, held_ref, out_ref, any_out,
    any_ref, ancs, lens, places, header, own, header_sems, live_sems, any_sem,
):
    del held_ref
    rows, _, slots, _ = out_ref.shape
    top = pl.ds(0, TILE)
    load_all(
        (anc_in, head_a.at[0, top], head_b.at[0, top], sent_a.at[0, top], sent_b.at[0, top]),
        (ancs, header.at[0], header.at[1], own.at[0], own.at[1]),
        header_sems,
    )
    read_headers(header, lens, places, steps, slots // TILE)

    def each(act):
        def one(child, side, count, place):
            for which, head in enumerate((head_a, head_b)):

                if side != which:
                    continue

                @pl.when(place + count <= HEAD)
                def _():
                    source = head.at[:, tiles(place, count)]
                    target = out_ref.at[child, :, tiles(0, count)]
                    act(pltpu.make_async_copy(source, target, live_sems.at[child]))

        remote_rows(ancs, lens, places, rows, one)

    each(lambda copy: copy.start())
    flag = rows // 2
    both = jnp.maximum(header[...].astype(F32), own[...].astype(F32))
    both = jnp.maximum(both[0, flag : flag + 1], both[1, flag : flag + 1])
    any_ref[0] = jnp.max(both).astype(jnp.int32)
    tell = pltpu.make_async_copy(any_ref, any_out, any_sem.at[0])
    tell.start()
    each(lambda copy: copy.wait())
    tell.wait()


def place(steps, ancestors, sent, heads, held):
    rows, _, _, hd = held.shape
    half = rows // 2
    return pl.pallas_call(
        functools.partial(place_kernel, steps),
        out_shape=(
            like(held),
            jax.ShapeDtypeStruct((1,), jnp.int32),
        ),
        in_specs=[ANY] * 5 + [HBM],
        out_specs=(HBM, HBM),
        scratch_shapes=[
            pltpu.SMEM((1,), jnp.int32),
            pltpu.SMEM((rows,), jnp.int32),
            pltpu.SMEM((2, half), jnp.int32),
            pltpu.SMEM((2, half), jnp.int32),
            pltpu.VMEM((2, TILE, hd), BF16),
            pltpu.VMEM((2, TILE, hd), BF16),
            pltpu.SemaphoreType.DMA((5,)),
            pltpu.SemaphoreType.DMA((rows,)),
            pltpu.SemaphoreType.DMA((1,)),
        ],
        input_output_aliases={5: 0},
        compiler_params=params(1),
        name="place",
    )(ancestors, *sent, *heads, in_hbm(held))


def place_tails_kernel(
    steps, anc_in, head_a, head_b, tail_a, tail_b, held_ref, out_ref,
    ancs, lens, places, header, header_sems, live_sems,
):
    del held_ref
    rows, _, slots, _ = out_ref.shape
    top = pl.ds(0, TILE)
    load_all(
        (anc_in, head_a.at[0, top], head_b.at[0, top]), (ancs, header.at[0], header.at[1]), header_sems
    )
    read_headers(header, lens, places, steps, slots // TILE)

    def each(act):
        def one(child, side, count, place):
            for which, tail in enumerate((tail_a, tail_b)):

                if side != which:
                    continue

                @pl.when(place + count > HEAD)
                def _():
                    source = tail.at[:, tiles(place - SLACK, count)]
                    target = out_ref.at[child, :, tiles(0, count)]
                    act(pltpu.make_async_copy(source, target, live_sems.at[child]))

        remote_rows(ancs, lens, places, rows, one)

    each(lambda copy: copy.start())
    each(lambda copy: copy.wait())


def place_tails(steps, ancestors, heads, tails, held):
    rows, _, _, hd = held.shape
    half = rows // 2
    return pl.pallas_call(
        functools.partial(place_tails_kernel, steps),
        out_shape=like(held),
        in_specs=[ANY] * 5 + [HBM],
        out_specs=HBM,
        scratch_shapes=[
            pltpu.SMEM((rows,), jnp.int32),
            pltpu.SMEM((2, half), jnp.int32),
            pltpu.SMEM((2, half), jnp.int32),
            pltpu.VMEM((2, TILE, hd), BF16),
            pltpu.SemaphoreType.DMA((3,)),
            pltpu.SemaphoreType.DMA((rows,)),
        ],
        input_output_aliases={5: 0},
        compiler_params=params(1),
        name="place_tails",
    )(ancestors, *heads, *tails, in_hbm(held))


def attend_kernel(
    len_in, cache_ref, nk_in, nv_in, q_ref, pk_ref, pv_ref, w_ref, theirs_ref, ours_ref, app_ref,
    len_ref, nk, nv, small_sems, in_sems, qs, att, wbuf, sems,
):
    rows, steps, _ = q_ref.shape
    heads = q_ref.shape[2] // HD
    slots = app_ref.shape[2]
    chips, tokens, width = theirs_ref.shape
    core = lax.rem(lax.axis_index("tp"), 2)

    def w_copy(k):
        who = jnp.where(k < chips, 1 - core, core)
        cols = pl.ds(pl.multiple_of((2 * lax.rem(k, chips) + who) * width, width), width)
        return pltpu.make_async_copy(w_ref.at[:, cols], wbuf.at[k], sems.at[k])

    @pl.loop(0, rows)
    def _(p):
        pltpu.make_async_copy(cache_ref.at[p], app_ref.at[p], in_sems.at[p]).start()

    @pl.loop(0, 2 * chips)
    def _(k):
        w_copy(k).start()

    load_all((len_in, nk_in, nv_in), (len_ref, nk, nv), small_sems)

    pair = 2 * steps
    groups = rows // 2
    block = heads * pair
    for g in range(groups):
        two = jnp.concatenate([q_ref[2 * g].astype(F32), q_ref[2 * g + 1].astype(F32)], 0)
        for h in range(heads):
            qs[pl.ds((g * heads + h) * pair, pair), :] = two[:, h * HD : (h + 1) * HD]

    for p in range(rows):
        pltpu.make_async_copy(cache_ref.at[p], app_ref.at[p], in_sems.at[p]).wait()
        count = live_tiles(len_ref[p], steps)
        for kv, fresh_ref in ((0, nk), (1, nv)):
            fresh = fresh_ref[p].astype(F32)
            for tile in (jnp.maximum(count - 2, 0), count - 1):
                insert(app_ref, (p, kv, tile_at(tile)), tile, len_ref[p], fresh, steps)

    factor = math.log2(math.e) / math.sqrt(HD)
    per = 4
    big = per * block
    prompt_k = pk_ref[...]
    prompt_v = pv_ref[...]
    r = lax.broadcasted_iota(jnp.int32, (pair, 2 * slots), 0)
    c = lax.broadcasted_iota(jnp.int32, (pair, 2 * slots), 1)
    same = (r // steps) == (c // slots)
    lead = jnp.where(same, lax.rem(c, slots) - lax.rem(r, steps), slots)
    left = c[:1] < slots
    nt = (((1,), (1,)), ((), ()))
    for ch in range(groups // per):
        q = qs[pl.ds(ch * big, big), :].astype(BF16)
        s_prompt = lax.dot_general(q, prompt_k, nt, preferred_element_type=F32)
        s_own = []
        for i in range(per):
            g = ch * per + i
            keys = app_ref[2 * g : 2 * g + 2, 0].reshape(2 * slots, HD)
            s = lax.dot_general(
                q[i * block : (i + 1) * block], keys, nt, preferred_element_type=F32
            )
            limit = jnp.where(left, len_ref[2 * g], len_ref[2 * g + 1])
            seen = lead <= limit
            s = s.reshape(heads, pair, 2 * slots)
            s_own.append(jnp.where(seen[None], s, -1e30).reshape(block, 2 * slots))
        s_own = jnp.concatenate(s_own, 0)
        top = jnp.maximum(
            jnp.max(s_prompt, axis=1, keepdims=True), jnp.max(s_own, axis=1, keepdims=True)
        )
        e_prompt = jnp.exp2((s_prompt - top) * factor)
        e_own = jnp.exp2((s_own - top) * factor)
        total = jnp.sum(e_prompt, axis=1, keepdims=True) + jnp.sum(e_own, axis=1, keepdims=True)
        o = jnp.dot(e_prompt.astype(BF16), prompt_v, preferred_element_type=F32)
        e_own = e_own.astype(BF16)
        own = []
        for i in range(per):
            g = ch * per + i
            values = app_ref[2 * g : 2 * g + 2, 1].reshape(2 * slots, HD)
            own.append(
                jnp.dot(
                    e_own[i * block : (i + 1) * block], values, preferred_element_type=F32
                )
            )
        o = (o + jnp.concatenate(own, 0)) / total
        for i in range(per):
            g = ch * per + i
            for h in range(heads):
                at = i * block + h * pair
                att[pl.ds(g * pair, pair), h * HD : (h + 1) * HD] = o[at : at + pair]

    attended = att[...].astype(BF16)
    for k in range(2 * chips):
        w_copy(jnp.int32(k)).wait()
        part = jnp.dot(attended, wbuf[k], preferred_element_type=F32)
        if k < chips:
            theirs_ref[k] = part.astype(BF16)
        else:
            ours_ref[k - chips] = part


def attend(
    lengths, cache, new_keys, new_values, queries, prompt_keys, prompt_values, out_weight, chips, width
):
    rows, steps, q_cols = queries.shape
    tokens = rows * steps
    flops = 2 * 2 * tokens * q_cols * prompt_keys.shape[0] + 2 * tokens * out_weight.size
    return pl.pallas_call(
        attend_kernel,
        out_shape=(
            jax.ShapeDtypeStruct((chips, tokens, width), BF16),
            jax.ShapeDtypeStruct((chips, tokens, width), F32),
            like(cache),
        ),
        in_specs=[ANY, HBM, ANY, ANY, VMEM, VMEM, VMEM, HBM],
        out_specs=(VMEM, VMEM, VMEM),
        scratch_shapes=[
            pltpu.SMEM((rows,), jnp.int32),
            pltpu.VMEM(new_keys.shape, BF16),
            pltpu.VMEM(new_values.shape, BF16),
            pltpu.SemaphoreType.DMA((3,)),
            pltpu.SemaphoreType.DMA((rows,)),
            pltpu.VMEM((tokens * q_cols // HD, HD), F32),
            pltpu.VMEM((tokens, q_cols), F32),
            pltpu.VMEM((2 * chips, out_weight.shape[0], width), BF16),
            pltpu.SemaphoreType.DMA((2 * chips,)),
        ],
        compiler_params=params(40),
        cost_estimate=pl.CostEstimate(
            flops=flops, bytes_accessed=2 * out_weight.size, transcendentals=0
        ),
        name="attend",
    )(
        lengths, in_hbm(cache), new_keys, new_values, queries, prompt_keys, prompt_values,
        in_hbm(out_weight),
    )


def pair_sum_kernel(ours_ref, got_ref, keep_ref, *send_refs):
    chips = ours_ref.shape[0]
    me = lax.axis_index("tp") // 2
    for k in range(chips):
        at = lax.rem(me + k, chips)
        both = ours_ref[at] + got_ref[at].astype(F32)
        if k == 0:
            keep_ref[...] = both
        else:
            send_refs[k - 1][...] = both.astype(BF16)


def pair_sum(ours, got):
    chips, tokens, width = ours.shape
    return pl.pallas_call(
        pair_sum_kernel,
        out_shape=(jax.ShapeDtypeStruct((tokens, width), F32),)
        + (jax.ShapeDtypeStruct((tokens, width), BF16),) * (chips - 1),
        in_specs=[VMEM, VMEM],
        out_specs=(VMEM,) * chips,
        compiler_params=params(2),
        name="pair_sum",
    )(ours, got)


def chip_sum_kernel(keep_ref, *refs):
    got_refs, out_ref = refs[:-1], refs[-1]
    rows, steps, _ = out_ref.shape
    total = keep_ref[...]
    for ref in got_refs:
        total = total + ref[...].astype(F32)
    total = total.astype(BF16)
    for p in range(rows):
        out_ref[p] = total[p * steps : (p + 1) * steps]


def chip_sum(keep, got, rows):
    tokens, width = keep.shape
    return pl.pallas_call(
        chip_sum_kernel,
        out_shape=jax.ShapeDtypeStruct((rows, tokens // rows, width), BF16),
        in_specs=[VMEM] * (1 + len(got)),
        out_specs=VMEM,
        compiler_params=params(2),
        name="chip_sum",
    )(keep, *got)


def body(
    queries,
    new_keys,
    new_values,
    prompt_keys,
    prompt_values,
    suffix_cache,
    lengths,
    ancestors,
    out_weight,
):
    rows, steps, _ = queries.shape
    doms = lax.axis_size("dom")
    tps = lax.axis_size("tp")
    chips = tps // 2
    width = out_weight.shape[1] // tps

    packed = first(lengths, suffix_cache, new_keys, new_values)
    def partner(i, side):
        dom, tp = divmod(i, tps)
        other = dom ^ 1 if side == 0 else (dom + 1) // 2 * 4 - 1 - dom
        return other * tps + tp if 0 <= other < doms else i ^ 1

    routes = [[(i, partner(i, side)) for i in range(doms * tps)] for side in range(2)]
    heads = [lax.ppermute(head, ("dom", "tp"), route) for head, route in zip(packed[:2], routes)]

    theirs, ours, app = attend(
        lengths, suffix_cache, new_keys, new_values, queries, prompt_keys, prompt_values, out_weight,
        chips, width,
    )
    got = lax.ppermute(theirs, "tp", [(i, i ^ 1) for i in range(tps)])
    mine, *send = pair_sum(ours, got)
    arrived = [
        lax.ppermute(send[k - 1], "tp", [(i, (i + 2 * k) % tps) for i in range(tps)])
        for k in (2, 3, 1)
    ]
    mixed = chip_sum(mine, arrived, rows)
    held = keep(steps, lengths, ancestors, app)

    held, some = place(steps, ancestors, packed[:2], heads, held)

    def exchange(held, *tails):
        more = [
            jnp.maximum(sent[0, rows // 2, 0], got[0, rows // 2, 0])
            for sent, got in zip(packed[:2], heads)
        ]
        got = [
            lax.cond(
                flag > 0, lambda v, route=route: lax.ppermute(v, ("dom", "tp"), route), lambda v: v, tail
            )
            for flag, tail, route in zip(more, tails, routes)
        ]
        return place_tails(steps, ancestors, heads, got, held)

    new_cache = lax.cond(some[0] > 0, exchange, lambda held, *tails: held, held, *packed[2:])
    return (mixed, new_cache)


def solution(mesh):
    in_specs = (
        P("dom", None, "tp"),
        P("dom", None, "tp"),
        P("dom", None, "tp"),
        P(None, "tp"),
        P(None, "tp"),
        P("dom", None, None, "tp"),
        P("dom"),
        P("dom"),
        P("tp", None),
    )
    out_specs = (P("dom", None, "tp"), P("dom", None, None, "tp"))
    return jax.shard_map(body, mesh=mesh, in_specs=in_specs, out_specs=out_specs, check_vma=False)
```

```python
import functools
import math

import jax
import jax.numpy as jnp
from jax import lax
from jax.experimental import pallas as pl
from jax.experimental.pallas import tpu as pltpu
from jax.sharding import PartitionSpec as P

HD = 128
TILE = 16
HEAD = 109
SLACK = HEAD - 15
F32 = jnp.float32
BF16 = jnp.bfloat16
VMEM = pl.BlockSpec(memory_space=pltpu.VMEM)
SMEM = pl.BlockSpec(memory_space=pltpu.SMEM)
HBM = pl.BlockSpec(memory_space=pltpu.HBM)
ANY = pl.BlockSpec(memory_space=pl.ANY)


def params(mib):
    return pltpu.CompilerParams(vmem_limit_bytes=mib * 1024 * 1024)


def in_hbm(value):
    return pltpu.with_memory_space_constraint(value, pltpu.HBM)


def like(value):
    return jax.ShapeDtypeStruct(value.shape, value.dtype)


def live_tiles(length, steps):
    return (length + steps + TILE - 1) // TILE


def tiles(first, count):
    return pl.ds(pl.multiple_of(first * TILE, TILE), pl.multiple_of(count * TILE, TILE))


def own_base(side, rows):
    even = lax.rem(lax.axis_index("dom"), 2) == 0
    return jnp.where(even, rows // 2 * (1 - side), rows // 2 * side)


def partner_of(side):
    me = lax.axis_index("dom")
    even = lax.rem(me, 2) == 0
    return jnp.where(even, me + 1 - 2 * side, me - 1 + 2 * side)


def assign(lens, base, places, steps):
    used = jnp.int32(1)
    for r in range(places.shape[0]):
        places[r] = used
        used = used + live_tiles(lens[base + r], steps)
    return used


def load_all(sources, targets, sems):
    copies = [
        pltpu.make_async_copy(a, b, sems.at[i]) for i, (a, b) in enumerate(zip(sources, targets))
    ]
    for copy in copies:
        copy.start()
    for copy in copies:
        copy.wait()


def tile_at(tile):
    return pl.ds(pl.multiple_of(tile * TILE, TILE), TILE)


def insert(target, at, tile, length, fresh, steps):
    line = lax.broadcasted_iota(jnp.int32, (TILE, HD), 0) + (tile * TILE - length)
    rows = target[at].astype(F32)
    for t in range(steps):
        rows = jnp.where(line == t, fresh[t : t + 1], rows)
    target[at] = jnp.where(line >= steps, 0.0, rows).astype(BF16)


def first_kernel(
    len_hbm, cache_ref, nk_hbm, nv_hbm, head_a, head_b, tail_a, tail_b,
    lens, nk, nv, place_a, place_b, spare, sems, head_sems, spare_sem,
):
    rows, kinds, slots, hd = cache_ref.shape
    half = rows // 2
    steps = nk.shape[1]
    copies = [
        pltpu.make_async_copy(a, b, sems.at[i])
        for i, (a, b) in enumerate(((len_hbm, lens), (nk_hbm, nk), (nv_hbm, nv)))
    ]
    for copy in copies:
        copy.start()
    copies[0].wait()
    sides = []
    for side, places, head, tail in ((0, place_a, head_a, tail_a), (1, place_b, head_b, tail_b)):
        base = own_base(side, rows)
        sides.append((side, base, assign(lens, base, places, steps), places, head, tail))

    def spots():
        for side, base, _, places, head, _ in sides:
            for r in range(half):
                count = live_tiles(lens[base + r], steps)
                copy = pltpu.make_async_copy(
                    cache_ref.at[base + r, :, tiles(0, count)],
                    head.at[:, tiles(places[r], count)],
                    head_sems.at[side, r],
                )
                yield places[r] + count <= HEAD, copy, base + r, count, places[r], head

    for fits, copy, *_ in spots():

        @pl.when(fits)
        def _():
            copy.start()

    for _, base, used, _, head, _ in sides:
        line = lax.broadcasted_iota(jnp.int32, (TILE, hd), 0)
        words = jnp.where(line == half, (used > HEAD).astype(jnp.int32), 0)
        for r in range(half):
            words = jnp.where(line == r, lens[base + r], words)
        head[0, :TILE, :] = words.astype(F32).astype(BF16)
    for copy in copies[1:]:
        copy.wait()

    def renew(target, place, p, count):
        def one(tile):
            for kv, fresh_ref in ((0, nk), (1, nv)):
                fresh = fresh_ref[p].astype(F32)
                insert(target, (kv, tile_at(place + tile)), tile, lens[p], fresh, steps)

        one(count - 1)

        @pl.when(lens[p] < (count - 1) * TILE)
        def _():
            one(count - 2)

    for fits, copy, p, count, place, head in spots():

        @pl.when(fits)
        def _():
            copy.wait()
            renew(head, place, p, count)

    for _, base, used, places, _, tail in sides:

        @pl.when(used > HEAD)
        def _():
            for r in range(half):
                count = live_tiles(lens[base + r], steps)
                place = places[r]

                @pl.when(place + count > HEAD)
                def _():
                    bring = pltpu.make_async_copy(cache_ref.at[base + r], spare, spare_sem.at[0])
                    bring.start()
                    bring.wait()
                    renew(spare, 0, base + r, count)
                    source = spare.at[:, tiles(0, count)]
                    target = tail.at[:, tiles(place - SLACK, count)]
                    leave = pltpu.make_async_copy(source, target, spare_sem.at[0])
                    leave.start()
                    leave.wait()


def first(lengths, cache, new_keys, new_values):
    rows, kinds, slots, hd = cache.shape
    half = rows // 2
    args = (lengths, cache, new_keys, new_values)
    head = jax.ShapeDtypeStruct((kinds, HEAD * TILE, hd), BF16)
    tail = jax.ShapeDtypeStruct((kinds, (half * slots // TILE + 1 - SLACK) * TILE, hd), BF16)
    return pl.pallas_call(
        first_kernel,
        out_shape=(
            head, head, tail, tail,
        ),
        in_specs=[HBM] * len(args),
        out_specs=(VMEM,) * 2 + (HBM,) * 2,
        scratch_shapes=[
            pltpu.SMEM((rows,), jnp.int32),
            pltpu.VMEM(new_keys.shape, BF16),
            pltpu.VMEM(new_values.shape, BF16),
            pltpu.SMEM((half,), jnp.int32),
            pltpu.SMEM((half,), jnp.int32),
            pltpu.VMEM(cache.shape[1:], BF16),
            pltpu.SemaphoreType.DMA((3,)),
            pltpu.SemaphoreType.DMA((2, half)),
            pltpu.SemaphoreType.DMA((1,)),
        ],
        compiler_params=params(4),
        name="first",
    )(*map(in_hbm, args))


def keep_kernel(steps, len_in, anc_in, app_ref, out_ref, lens, ancs, zero, live_sems, zero_sems, sems):
    rows, _, slots, _ = out_ref.shape
    first = lax.axis_index("dom") * rows
    zero[...] = jnp.zeros_like(zero)
    load_all((len_in, anc_in), (lens, ancs), sems)

    def each(act):
        @pl.loop(0, rows)
        def _(child):
            row = ancs[child] - first
            here = jnp.logical_and(row >= 0, row < rows)
            at = jnp.clip(row, 0, rows - 1)
            count = jnp.where(here, live_tiles(lens[at], steps), 0)
            rest = slots // TILE - count

            @pl.when(here)
            def _():
                part = tiles(0, count)
                source = app_ref.at[at, :, part]
                act(pltpu.make_async_copy(source, out_ref.at[child, :, part], live_sems.at[child]))

            @pl.when(rest > 0)
            def _():
                source = zero.at[:, tiles(0, rest)]
                target = out_ref.at[child, :, tiles(count, rest)]
                act(pltpu.make_async_copy(source, target, zero_sems.at[child]))

    each(lambda copy: copy.start())
    each(lambda copy: copy.wait())


def keep(steps, lengths, ancestors, app):
    rows = app.shape[0]
    return pl.pallas_call(
        functools.partial(keep_kernel, steps),
        out_shape=like(app),
        in_specs=[ANY, ANY, VMEM],
        out_specs=HBM,
        scratch_shapes=[
            pltpu.SMEM((rows,), jnp.int32),
            pltpu.SMEM((rows,), jnp.int32),
            pltpu.VMEM(app.shape[1:], BF16),
            pltpu.SemaphoreType.DMA((rows,)),
            pltpu.SemaphoreType.DMA((rows,)),
            pltpu.SemaphoreType.DMA((2,)),
        ],
        compiler_params=params(1),
        name="keep",
    )(lengths, ancestors, app)


def remote_rows(ancs, lens, places, rows, act):
    half = rows // 2
    me = lax.axis_index("dom")
    for side in range(2):
        partner = partner_of(side)
        children = jnp.where(partner > me, half, 0)
        for i in range(half):
            child = children + i
            row = ancs[child] - partner * rows - (half - children)

            @pl.when(jnp.logical_and(row >= 0, row < half))
            def _():
                act(child, side, lens[side, row], places[side, row])


def read_headers(header, lens, places, steps, most):
    half = lens.shape[1]
    for side in range(2):
        words = header[side].astype(F32)
        used = jnp.int32(1)
        for r in range(half):
            length = jnp.max(words[r : r + 1]).astype(jnp.int32)
            count = jnp.clip(live_tiles(length, steps), 1, most)
            lens[side, r] = count
            places[side, r] = used
            used = used + count


def place_kernel(
    steps, anc_in, sent_a, sent_b, head_a, head_b, held_ref, out_ref, any_out,
    any_ref, ancs, lens, places, header, own, header_sems, live_sems, any_sem,
):
    del held_ref
    rows, _, slots, _ = out_ref.shape
    top = pl.ds(0, TILE)
    load_all(
        (anc_in, head_a.at[0, top], head_b.at[0, top], sent_a.at[0, top], sent_b.at[0, top]),
        (ancs, header.at[0], header.at[1], own.at[0], own.at[1]),
        header_sems,
    )
    read_headers(header, lens, places, steps, slots // TILE)

    def each(act):
        def one(child, side, count, place):
            for which, head in enumerate((head_a, head_b)):

                if side != which:
                    continue

                @pl.when(place + count <= HEAD)
                def _():
                    source = head.at[:, tiles(place, count)]
                    target = out_ref.at[child, :, tiles(0, count)]
                    act(pltpu.make_async_copy(source, target, live_sems.at[child]))

        remote_rows(ancs, lens, places, rows, one)

    each(lambda copy: copy.start())
    flag = rows // 2
    both = jnp.maximum(header[...].astype(F32), own[...].astype(F32))
    both = jnp.maximum(both[0, flag : flag + 1], both[1, flag : flag + 1])
    any_ref[0] = jnp.max(both).astype(jnp.int32)
    tell = pltpu.make_async_copy(any_ref, any_out, any_sem.at[0])
    tell.start()
    each(lambda copy: copy.wait())
    tell.wait()


def place(steps, ancestors, sent, heads, held):
    rows, _, _, hd = held.shape
    half = rows // 2
    return pl.pallas_call(
        functools.partial(place_kernel, steps),
        out_shape=(
            like(held),
            jax.ShapeDtypeStruct((1,), jnp.int32),
        ),
        in_specs=[ANY] * 5 + [HBM],
        out_specs=(HBM, HBM),
        scratch_shapes=[
            pltpu.SMEM((1,), jnp.int32),
            pltpu.SMEM((rows,), jnp.int32),
            pltpu.SMEM((2, half), jnp.int32),
            pltpu.SMEM((2, half), jnp.int32),
            pltpu.VMEM((2, TILE, hd), BF16),
            pltpu.VMEM((2, TILE, hd), BF16),
            pltpu.SemaphoreType.DMA((5,)),
            pltpu.SemaphoreType.DMA((rows,)),
            pltpu.SemaphoreType.DMA((1,)),
        ],
        input_output_aliases={5: 0},
        compiler_params=params(1),
        name="place",
    )(ancestors, *sent, *heads, in_hbm(held))


def place_tails_kernel(
    steps, anc_in, head_a, head_b, tail_a, tail_b, held_ref, out_ref,
    ancs, lens, places, header, header_sems, live_sems,
):
    del held_ref
    rows, _, slots, _ = out_ref.shape
    top = pl.ds(0, TILE)
    load_all(
        (anc_in, head_a.at[0, top], head_b.at[0, top]), (ancs, header.at[0], header.at[1]), header_sems
    )
    read_headers(header, lens, places, steps, slots // TILE)

    def each(act):
        def one(child, side, count, place):
            for which, tail in enumerate((tail_a, tail_b)):

                if side != which:
                    continue

                @pl.when(place + count > HEAD)
                def _():
                    source = tail.at[:, tiles(place - SLACK, count)]
                    target = out_ref.at[child, :, tiles(0, count)]
                    act(pltpu.make_async_copy(source, target, live_sems.at[child]))

        remote_rows(ancs, lens, places, rows, one)

    each(lambda copy: copy.start())
    each(lambda copy: copy.wait())


def place_tails(steps, ancestors, heads, tails, held):
    rows, _, _, hd = held.shape
    half = rows // 2
    return pl.pallas_call(
        functools.partial(place_tails_kernel, steps),
        out_shape=like(held),
        in_specs=[ANY] * 5 + [HBM],
        out_specs=HBM,
        scratch_shapes=[
            pltpu.SMEM((rows,), jnp.int32),
            pltpu.SMEM((2, half), jnp.int32),
            pltpu.SMEM((2, half), jnp.int32),
            pltpu.VMEM((2, TILE, hd), BF16),
            pltpu.SemaphoreType.DMA((3,)),
            pltpu.SemaphoreType.DMA((rows,)),
        ],
        input_output_aliases={5: 0},
        compiler_params=params(1),
        name="place_tails",
    )(ancestors, *heads, *tails, in_hbm(held))


def attend_kernel(
    len_in, cache_ref, nk_in, nv_in, q_in, pk_in, pv_in, w_ref, theirs_ref, ours_ref, app_ref,
    len_ref, nk, nv, q_ref, pk_ref, pv_ref, small_sems, in_sems, qs, att, wbuf, sems,
):
    rows, steps, _ = q_ref.shape
    heads = q_ref.shape[2] // HD
    slots = app_ref.shape[2]
    chips, tokens, width = theirs_ref.shape
    core = lax.rem(lax.axis_index("tp"), 2)

    def w_copy(k):
        who = jnp.where(k < chips, 1 - core, core)
        cols = pl.ds(pl.multiple_of((2 * lax.rem(k, chips) + who) * width, width), width)
        return pltpu.make_async_copy(w_ref.at[:, cols], wbuf.at[k], sems.at[k])

    sources = (len_in, nk_in, nv_in, q_in, pk_in, pv_in)
    targets = (len_ref, nk, nv, q_ref, pk_ref, pv_ref)
    copies = [
        pltpu.make_async_copy(a, b, small_sems.at[i]) for i, (a, b) in enumerate(zip(sources, targets))
    ]
    for copy in copies:
        copy.start()

    @pl.loop(0, rows)
    def _(p):
        pltpu.make_async_copy(cache_ref.at[p], app_ref.at[p], in_sems.at[p]).start()

    @pl.loop(0, 2 * chips)
    def _(k):
        w_copy(k).start()

    for copy in copies:
        copy.wait()

    pair = 2 * steps
    groups = rows // 2
    block = heads * pair
    for g in range(groups):
        two = jnp.concatenate([q_ref[2 * g].astype(F32), q_ref[2 * g + 1].astype(F32)], 0)
        for h in range(heads):
            qs[pl.ds((g * heads + h) * pair, pair), :] = two[:, h * HD : (h + 1) * HD]

    for p in range(rows):
        pltpu.make_async_copy(cache_ref.at[p], app_ref.at[p], in_sems.at[p]).wait()
        count = live_tiles(len_ref[p], steps)
        for kv, fresh_ref in ((0, nk), (1, nv)):
            fresh = fresh_ref[p].astype(F32)
            for tile in (jnp.maximum(count - 2, 0), count - 1):
                insert(app_ref, (p, kv, tile_at(tile)), tile, len_ref[p], fresh, steps)

    factor = math.log2(math.e) / math.sqrt(HD)
    per = 4
    big = per * block
    prompt_k = pk_ref[...]
    prompt_v = pv_ref[...]
    r = lax.broadcasted_iota(jnp.int32, (pair, 2 * slots), 0)
    c = lax.broadcasted_iota(jnp.int32, (pair, 2 * slots), 1)
    same = (r // steps) == (c // slots)
    lead = jnp.where(same, lax.rem(c, slots) - lax.rem(r, steps), slots)
    left = c[:1] < slots
    nt = (((1,), (1,)), ((), ()))
    for ch in range(groups // per):
        q = qs[pl.ds(ch * big, big), :].astype(BF16)
        s_prompt = lax.dot_general(q, prompt_k, nt, preferred_element_type=F32)
        s_own = []
        for i in range(per):
            g = ch * per + i
            keys = app_ref[2 * g : 2 * g + 2, 0].reshape(2 * slots, HD)
            s = lax.dot_general(
                q[i * block : (i + 1) * block], keys, nt, preferred_element_type=F32
            )
            limit = jnp.where(left, len_ref[2 * g], len_ref[2 * g + 1])
            seen = lead <= limit
            s = s.reshape(heads, pair, 2 * slots)
            s_own.append(jnp.where(seen[None], s, -1e30).reshape(block, 2 * slots))
        s_own = jnp.concatenate(s_own, 0)
        top = jnp.maximum(
            jnp.max(s_prompt, axis=1, keepdims=True), jnp.max(s_own, axis=1, keepdims=True)
        )
        e_prompt = jnp.exp2((s_prompt - top) * factor)
        e_own = jnp.exp2((s_own - top) * factor)
        total = jnp.sum(e_prompt, axis=1, keepdims=True) + jnp.sum(e_own, axis=1, keepdims=True)
        o = jnp.dot(e_prompt.astype(BF16), prompt_v, preferred_element_type=F32)
        e_own = e_own.astype(BF16)
        own = []
        for i in range(per):
            g = ch * per + i
            values = app_ref[2 * g : 2 * g + 2, 1].reshape(2 * slots, HD)
            own.append(
                jnp.dot(
                    e_own[i * block : (i + 1) * block], values, preferred_element_type=F32
                )
            )
        o = (o + jnp.concatenate(own, 0)) / total
        for i in range(per):
            g = ch * per + i
            for h in range(heads):
                at = i * block + h * pair
                att[pl.ds(g * pair, pair), h * HD : (h + 1) * HD] = o[at : at + pair]

    attended = att[...].astype(BF16)
    for k in range(2 * chips):
        w_copy(jnp.int32(k)).wait()
        part = jnp.dot(attended, wbuf[k], preferred_element_type=F32)
        if k < chips:
            theirs_ref[k] = part.astype(BF16)
        else:
            ours_ref[k - chips] = part


def attend(
    lengths, cache, new_keys, new_values, queries, prompt_keys, prompt_values, out_weight, chips, width
):
    rows, steps, q_cols = queries.shape
    tokens = rows * steps
    flops = 2 * 2 * tokens * q_cols * prompt_keys.shape[0] + 2 * tokens * out_weight.size
    return pl.pallas_call(
        attend_kernel,
        out_shape=(
            jax.ShapeDtypeStruct((chips, tokens, width), BF16),
            jax.ShapeDtypeStruct((chips, tokens, width), F32),
            like(cache),
        ),
        in_specs=[HBM] * 8,
        out_specs=(VMEM, VMEM, VMEM),
        scratch_shapes=[
            pltpu.SMEM((rows,), jnp.int32),
            pltpu.VMEM(new_keys.shape, BF16),
            pltpu.VMEM(new_values.shape, BF16),
            pltpu.VMEM(queries.shape, BF16),
            pltpu.VMEM(prompt_keys.shape, BF16),
            pltpu.VMEM(prompt_values.shape, BF16),
            pltpu.SemaphoreType.DMA((6,)),
            pltpu.SemaphoreType.DMA((rows,)),
            pltpu.VMEM((tokens * q_cols // HD, HD), F32),
            pltpu.VMEM((tokens, q_cols), F32),
            pltpu.VMEM((2 * chips, out_weight.shape[0], width), BF16),
            pltpu.SemaphoreType.DMA((2 * chips,)),
        ],
        compiler_params=params(40),
        cost_estimate=pl.CostEstimate(
            flops=flops, bytes_accessed=2 * out_weight.size, transcendentals=0
        ),
        name="attend",
    )(
        *map(
            in_hbm,
            (
                lengths, cache, new_keys, new_values, queries, prompt_keys, prompt_values, out_weight,
            ),
        )
    )


def pair_sum_kernel(ours_ref, got_ref, keep_ref, *send_refs):
    chips = ours_ref.shape[0]
    me = lax.axis_index("tp") // 2
    for k in range(chips):
        at = lax.rem(me + k, chips)
        both = ours_ref[at] + got_ref[at].astype(F32)
        if k == 0:
            keep_ref[...] = both
        else:
            send_refs[k - 1][...] = both.astype(BF16)


def pair_sum(ours, got):
    chips, tokens, width = ours.shape
    return pl.pallas_call(
        pair_sum_kernel,
        out_shape=(jax.ShapeDtypeStruct((tokens, width), F32),)
        + (jax.ShapeDtypeStruct((tokens, width), BF16),) * (chips - 1),
        in_specs=[VMEM, VMEM],
        out_specs=(VMEM,) * chips,
        compiler_params=params(2),
        name="pair_sum",
    )(ours, got)


def chip_sum_kernel(keep_ref, *refs):
    got_refs, out_ref = refs[:-1], refs[-1]
    rows, steps, _ = out_ref.shape
    total = keep_ref[...]
    for ref in got_refs:
        total = total + ref[...].astype(F32)
    total = total.astype(BF16)
    for p in range(rows):
        out_ref[p] = total[p * steps : (p + 1) * steps]


def chip_sum(keep, got, rows):
    tokens, width = keep.shape
    return pl.pallas_call(
        chip_sum_kernel,
        out_shape=jax.ShapeDtypeStruct((rows, tokens // rows, width), BF16),
        in_specs=[VMEM] * (1 + len(got)),
        out_specs=VMEM,
        compiler_params=params(2),
        name="chip_sum",
    )(keep, *got)


def body(
    queries,
    new_keys,
    new_values,
    prompt_keys,
    prompt_values,
    suffix_cache,
    lengths,
    ancestors,
    out_weight,
):
    rows, steps, _ = queries.shape
    doms = lax.axis_size("dom")
    tps = lax.axis_size("tp")
    chips = tps // 2
    width = out_weight.shape[1] // tps

    packed = first(lengths, suffix_cache, new_keys, new_values)
    def partner(i, side):
        dom, tp = divmod(i, tps)
        other = dom ^ 1 if side == 0 else (dom + 1) // 2 * 4 - 1 - dom
        return other * tps + tp if 0 <= other < doms else i ^ 1

    routes = [[(i, partner(i, side)) for i in range(doms * tps)] for side in range(2)]
    heads = [lax.ppermute(head, ("dom", "tp"), route) for head, route in zip(packed[:2], routes)]

    theirs, ours, app = attend(
        lengths, suffix_cache, new_keys, new_values, queries, prompt_keys, prompt_values, out_weight,
        chips, width,
    )
    got = lax.ppermute(theirs, "tp", [(i, i ^ 1) for i in range(tps)])
    mine, *send = pair_sum(ours, got)
    arrived = [
        lax.ppermute(send[k - 1], "tp", [(i, (i + 2 * k) % tps) for i in range(tps)])
        for k in (2, 3, 1)
    ]
    mixed = chip_sum(mine, arrived, rows)
    held = keep(steps, lengths, ancestors, app)

    held, some = place(steps, ancestors, packed[:2], heads, held)

    def exchange(held, *tails):
        more = [
            jnp.maximum(sent[0, rows // 2, 0], got[0, rows // 2, 0])
            for sent, got in zip(packed[:2], heads)
        ]
        got = [
            lax.cond(
                flag > 0, lambda v, route=route: lax.ppermute(v, ("dom", "tp"), route), lambda v: v, tail
            )
            for flag, tail, route in zip(more, tails, routes)
        ]
        return place_tails(steps, ancestors, heads, got, held)

    new_cache = lax.cond(some[0] > 0, exchange, lambda held, *tails: held, held, *packed[2:])
    return (mixed, new_cache)


def solution(mesh):
    in_specs = (
        P("dom", None, "tp"),
        P("dom", None, "tp"),
        P("dom", None, "tp"),
        P(None, "tp"),
        P(None, "tp"),
        P("dom", None, None, "tp"),
        P("dom"),
        P("dom"),
        P("tp", None),
    )
    out_specs = (P("dom", None, "tp"), P("dom", None, None, "tp"))
    return jax.shard_map(body, mesh=mesh, in_specs=in_specs, out_specs=out_specs, check_vma=False)
```
